32 devices in a mesh: section: 2 (over x), mp: 16 (over z, y, core).
Axes of the slice: x: 2, y: 2, z: 4, core: 2. Of those that a mesh axis runs over, the one named last changes fastest.
Arguments:
- enc_final: bfloat16 [2, 128, 4096], P('section', None, 'mp'), may hold values from -64 to 64
- enc_len: int32 [2], replicated, may hold values from 32 to 128, as said below
- kv_weight: bfloat16 [2, 4096, 2, 4096], P('section', None, None, 'mp'), may hold values from -1 to 1
- queries: bfloat16 [2, 2, 512, 4096], P('section', None, None, 'mp'), may hold values from -4096 to 4096
- d_context: bfloat16 [2, 2, 512, 4096], P('section', None, None, 'mp'), may hold values from -6 to 6
Outputs:
- context: bfloat16 [2, 2, 512, 4096], P('section', None, None, 'mp')
- query_grad: bfloat16 [2, 2, 512, 4096], P('section', None, None, 'mp')
- kv_weight_grad: bfloat16 [2, 4096, 2, 4096], P('section', None, None, 'mp')
- enc_grad: bfloat16 [2, 128, 4096], P('section', None, 'mp')
The draws below stay inside these ranges and needn't reach their ends.
Inputs may be any that keep to these rules, and one draw needn't show every extreme that they name: `enc_len`: some microbatch has exactly 128 valid positions.
All inputs are finite; a program needn't handle non-finite values.
Results may differ from the reference program's by a relative error of at most 0.02.
Values may be sent and summed in bfloat16 or wider, within the bound.
A program may use at most 128 MiB of HBM per device.

```python
import jax
import jax.numpy as jnp
from jax import lax

D = 4096
HEADS = 64
HD = 64
SRC = 128
TGT = 512
MICRO = 2
N_SECTION = 2


def encoder_draw(key):
    drawn = jnp.clip(jax.random.normal(jax.random.fold_in(key, 101), (MICRO, SRC, D), jnp.float32), -6.0, 6.0)
    return drawn


def weight_draw(key):
    drawn = jnp.clip(jax.random.normal(jax.random.fold_in(key, 201), (N_SECTION, D, 2, D), jnp.float32), -6.0, 6.0)
    return drawn * D ** (-0.5)


def draw_enc_final(key, part):
    return encoder_draw(key).astype(jnp.bfloat16)


def draw_kv_weight(key, part):
    return weight_draw(key).astype(jnp.bfloat16)


def draw_enc_len(key, part):
    quarter = SRC // 4
    lengths = jax.random.randint(jax.random.fold_in(key, 601), (MICRO,), quarter, SRC)
    chosen = jax.random.randint(jax.random.fold_in(key, 602), (), 0, MICRO)
    lengths = lengths.at[chosen].set(SRC)
    return lengths.astype(jnp.int32)


def draw_queries(key, part):
    drawn = jnp.clip(jax.random.normal(jax.random.fold_in(key, 301), (N_SECTION, MICRO, TGT, D), jnp.float32), -6.0, 6.0)
    return drawn.astype(jnp.bfloat16)


def block_levels(key, dims, cuts, low, largest):
    def one(axis_at, parts):
        heights = jax.random.uniform(jax.random.fold_in(jax.random.fold_in(key, 6), axis_at), (parts,), jnp.float32, low / len(cuts), largest / len(cuts))
        return jnp.repeat(jnp.exp(heights), dims[axis_at] // parts).reshape((-1,) + (1,) * (len(dims) - axis_at - 1))

    loudness = one(*cuts[0])
    for cut in cuts[1:]:
        loudness = loudness * one(*cut)
    return loudness


def bell_draw(own_key, extent, scale, most, pieces=(), kind=jnp.bfloat16):
    gain = block_levels(own_key, extent, pieces, -0.22, 0.18) if pieces else 1.0
    array = jax.random.normal(own_key, extent, jnp.float32) * scale * gain
    return jnp.minimum(jnp.maximum(array, -most), most).astype(kind)


def setup_inputs(seed: int = 0) -> dict:
    key_of = jax.random.split(jax.random.key(seed), 6)
    enc_final = draw_enc_final(jax.random.fold_in(key_of[5], 71), 0)
    enc_len = draw_enc_len(jax.random.fold_in(key_of[5], 71), 0)
    kv_weight = draw_kv_weight(jax.random.fold_in(key_of[5], 71), 0)
    queries = draw_queries(jax.random.fold_in(key_of[5], 71), 0)
    d_context = bell_draw(key_of[4], (N_SECTION, MICRO, TGT, D), 1.0, 6.0, ((0, 2), (3, 16)))
    return {"enc_final": enc_final, "enc_len": enc_len, "kv_weight": kv_weight, "queries": queries, "d_context": d_context}


def layer_terms(enc_flat, valid_key, weight, query_in, grad_in):
    weight_flat = weight.reshape(D, 2 * D)
    key_value = jnp.dot(enc_flat, weight_flat, preferred_element_type=jnp.float32).astype(jnp.bfloat16)
    key_value = lax.optimization_barrier(key_value).astype(jnp.float32).reshape(MICRO, SRC, 2, HEADS, HD)
    key_heads = key_value[:, :, 0]
    value_heads = key_value[:, :, 1]
    query_heads = query_in.reshape(MICRO, TGT, HEADS, HD).astype(jnp.float32)
    grad_heads = grad_in.reshape(MICRO, TGT, HEADS, HD).astype(jnp.float32)
    factor = HD ** -0.5
    scores = jnp.einsum('mthd,mshd->mhts', query_heads, key_heads) * factor
    scores = jnp.where(valid_key[:, None, None, :], scores, -1e30)
    row_peak = jnp.max(scores, axis=-1, keepdims=True)
    exponent = jnp.exp(scores - row_peak)
    attn_prob = exponent / jnp.sum(exponent, axis=-1, keepdims=True)
    rounded = lax.optimization_barrier(attn_prob.astype(jnp.bfloat16)).astype(jnp.float32)
    context = jnp.einsum('mhts,mshd->mthd', rounded, value_heads).astype(jnp.bfloat16)
    value_grad = jnp.einsum('mhts,mthd->mshd', rounded, grad_heads)
    prob_grad = jnp.einsum('mthd,mshd->mhts', grad_heads, value_heads)
    score_grad = attn_prob * (prob_grad - jnp.sum(prob_grad * attn_prob, axis=-1, keepdims=True))
    score_rounded = lax.optimization_barrier((score_grad * factor).astype(jnp.bfloat16)).astype(jnp.float32)
    key_grad = jnp.einsum('mhts,mthd->mshd', score_rounded, query_heads)
    query_grad = jnp.einsum('mhts,mshd->mthd', score_rounded, key_heads).astype(jnp.bfloat16)
    kv_grad = jnp.stack([key_grad, value_grad], axis=2).astype(jnp.bfloat16).reshape(MICRO * SRC, 2 * D)
    weight_grad = lax.dot_general(enc_flat, kv_grad, (((0,), (0,)), ((), ())), preferred_element_type=jnp.float32).astype(jnp.bfloat16)
    enc_term = lax.dot_general(kv_grad, weight_flat, (((1,), (1,)), ((), ())), preferred_element_type=jnp.float32)
    return context.reshape(MICRO, TGT, D), query_grad.reshape(MICRO, TGT, D), weight_grad.reshape(D, 2, D), enc_term


def reference(enc_final, enc_len, kv_weight, queries, d_context):
    enc_flat = enc_final.reshape(MICRO * SRC, D)
    valid_key = jnp.arange(SRC, dtype=jnp.int32)[None, :] < enc_len[:, None]

    def advance(running, layer_in):
        weight, query_in, grad_in = layer_in
        context, query_grad, weight_grad, enc_term = layer_terms(enc_flat, valid_key, weight, query_in, grad_in)
        return running + enc_term, (context, query_grad, weight_grad)

    running, stacked = lax.scan(advance, jnp.zeros((MICRO * SRC, D), jnp.float32), (kv_weight, queries, d_context))
    context, query_grad, weight_grad = stacked
    return context, query_grad, weight_grad, running.reshape(MICRO, SRC, D).astype(jnp.bfloat16)
```

```python
import functools

import jax
import jax.numpy as jnp
from jax import lax
from jax.experimental import pallas as pl
from jax.experimental.pallas import tpu as pltpu
from jax.sharding import PartitionSpec as P

HD = 64
LANES = 128
MESH = pl.DeviceIdType.MESH
VMEM_BYTES = 56 * 2**20
NT = (((1,), (1,)), ((), ()))
TN = (((0,), (0,)), ((), ()))


def wrap(value, size):
    return lax.rem(value, size)


class Grid:
    def __init__(self, section, mp):
        self.S, self.M = section, mp
        self.C = 2 if mp % 2 == 0 else 1
        self.Y = 2 if (mp // self.C) % 2 == 0 else 1
        self.Z = mp // self.C // self.Y

    def here(self):
        x, p = lax.axis_index("section"), lax.axis_index("mp")
        c = lax.rem(p, self.C)
        zy = lax.div(p, self.C)
        return x, lax.div(zy, self.Y), lax.rem(zy, self.Y), c

    def p(self, z, y, c):
        return (z * self.Y + y) * self.C + c

    def tile(self, x, z, y, c):
        return x * self.M + self.p(z, y, c)

    def device(self, x, z, y, c):
        return (x, self.p(z, y, c))

    def barrier(self):
        x, z, y, c = self.here()
        sem = pltpu.get_barrier_semaphore()
        peers = [self.device(wrap(x + d, self.S), z, y, c) for d in range(1, self.S)]
        peers += [self.device(x, wrap(z + d, self.Z), y, c) for d in range(1, self.Z)]
        peers += [self.device(x, z, wrap(y + d, self.Y), c) for d in range(1, self.Y)]
        peers += [self.device(x, z, y, wrap(c + d, self.C)) for d in range(1, self.C)]
        for peer in peers:
            pl.semaphore_signal(sem, inc=1, device_id=peer, device_id_type=MESH)
        pl.semaphore_wait(sem, len(peers))


def each(low, high, body):
    def step(i, carry):
        body(i)
        return carry

    lax.fori_loop(low, high, step, 0)


def gather_kernel(
    grid, enc_ref, w_ref, states_ref, wcat_ref, kv_ref,
    held, weight, raw, wide, total, raw_sem, send_sem, recv_sem, out_sem,
):
    S, Y, Z, C = grid.S, grid.Y, grid.Z, grid.C
    R, F = enc_ref.shape
    depth = weight.shape[0]
    L = weight.shape[1] // 2
    lane_tiles = L // LANES
    x, z, y, c = grid.here()

    def fetch(j):
        return pltpu.make_async_copy(
            w_ref.at[:, :, pl.ds(j * LANES, LANES)], raw.at[j], raw_sem.at[j]
        )

    for j in range(lane_tiles):
        fetch(j).start()
    held[grid.tile(x, z, y, c)] = enc_ref[...]
    total[...] = jnp.zeros_like(total)
    grid.barrier()

    whole = pl.ds(0, R)
    upper, lower = pl.ds(0, R // 2), pl.ds(R // 2, R // 2)
    at_x = Z
    at_y = at_x + (S - 1) * Z
    at_a = at_y + (Y - 1) * Z
    at_b = at_a + (S - 1) * (Y - 1) * Z
    at_s = at_b + (S - 1) * (Y - 1) * Z

    def move(t, rows, target, slot, part=0):
        return pltpu.make_async_remote_copy(
            src_ref=held.at[t, rows],
            dst_ref=held.at[t, rows],
            send_sem=send_sem.at[slot],
            recv_sem=recv_sem.at[part, t],
            device_id=target,
            device_id_type=MESH,
        )

    def arrived(t, rows=whole, part=0):
        move(t, rows, grid.device(wrap(x + 1, S), z, y, c), 0, part).wait_recv()

    def to_sibling(t, dx, dy, dz):
        return [
            move(t, whole, grid.device(x, z, y, wrap(c + d, C)), at_s + (dx * Y + dy) * Z + dz)
            for d in range(1, C)
        ]

    def spread(dz):
        t = grid.tile(x, wrap(z + dz, Z), y, c)
        copies = [
            move(t, whole, grid.device(wrap(x + d, S), z, y, c), at_x + (d - 1) * Z + dz)
            for d in range(1, S)
        ]
        copies += [
            move(t, whole, grid.device(x, z, wrap(y + d, Y), c), at_y + (d - 1) * Z + dz)
            for d in range(1, Y)
        ]
        return copies + to_sibling(t, 0, 0, dz)

    def pass_x(dx, dz):
        t = grid.tile(wrap(x + dx, S), wrap(z + dz, Z), y, c)
        copies = [
            move(t, upper, grid.device(x, z, wrap(y + d, Y), c),
                 at_a + ((dx - 1) * (Y - 1) + d - 1) * Z + dz, 0)
            for d in range(1, Y)
        ]
        return copies + to_sibling(t, dx, 0, dz)

    def pass_y(dy, dz):
        t = grid.tile(x, wrap(z + dz, Z), wrap(y + dy, Y), c)
        copies = [
            move(t, lower, grid.device(wrap(x + d, S), z, y, c),
                 at_b + ((d - 1) * (Y - 1) + dy - 1) * Z + dz, 1)
            for d in range(1, S)
        ]
        return copies + to_sibling(t, 0, dy, dz)

    def start(copies):
        for copy in copies:
            copy.start()

    def done(copies):
        for copy in copies:
            copy.wait_send()

    own = grid.tile(x, z, y, c)

    def along_z(dz):
        return [move(own, whole, grid.device(x, wrap(z + dz, Z), y, c), dz)]

    each(1, Z, lambda dz: start(along_z(dz)))
    start(spread(0))

    def unpack(low, high):
        for j in range(lane_tiles):
            flat = raw.at[j].reshape(2 * depth, LANES)

            def block(i):
                row = pl.multiple_of(i * F, F)
                wide[...] = flat[pl.ds(pl.multiple_of(2 * i * F, 2 * F), 2 * F), :].astype(
                    jnp.float32
                )
                for kind in range(2):
                    first = kind * L + j * LANES
                    weight[pl.ds(row, F), first : first + LANES] = wide[
                        pl.ds(kind, F, stride=2), :
                    ].astype(jnp.bfloat16)

            each(low, high, block)

    blocks = depth // F
    for j in range(lane_tiles):
        fetch(j).wait()
    unpack(0, blocks // 2)

    def column(dz):
        arrived(grid.tile(x, wrap(z + dz, Z), y, c))
        start(spread(dz))

    each(1, Z, column)
    unpack(blocks // 2, blocks)
    weight_out = pltpu.make_async_copy(weight, wcat_ref, out_sem.at[0])
    weight_out.start()

    def multiply(tx, tz, ty, tc):
        row = pl.multiple_of(grid.p(tz, ty, tc) * F, F)
        total[tx] += jnp.dot(
            held[grid.tile(tx, tz, ty, tc)],
            weight[pl.ds(row, F), :],
            preferred_element_type=jnp.float32,
        )

    def sides(dz):
        tz = wrap(z + dz, Z)
        for dx in range(1, S):
            arrived(grid.tile(wrap(x + dx, S), tz, y, c))
            start(pass_x(dx, dz))
        for dy in range(1, Y):
            arrived(grid.tile(x, tz, wrap(y + dy, Y), c))
            start(pass_y(dy, dz))
        multiply(x, tz, y, c)

    each(0, Z, sides)

    def diagonal(dz):
        tz = wrap(z + dz, Z)
        for dx in range(1, S):
            for dy in range(1, Y):
                tx, ty = wrap(x + dx, S), wrap(y + dy, Y)
                t = grid.tile(tx, tz, ty, c)
                arrived(t, upper, 0)
                arrived(t, lower, 1)
                start(to_sibling(t, dx, dy, dz))
        for dx in range(1, S):
            multiply(wrap(x + dx, S), tz, y, c)
        for dy in range(1, Y):
            multiply(x, tz, wrap(y + dy, Y), c)

    each(0, Z, diagonal)

    def rest(dz):
        tz = wrap(z + dz, Z)
        for dx in range(1, S):
            for dy in range(1, Y):
                multiply(wrap(x + dx, S), tz, wrap(y + dy, Y), c)

    each(0, Z, rest)

    for dc in range(1, C):
        for dx in range(S):
            for dy in range(Y):

                def other(dz):
                    tx, tz, ty = wrap(x + dx, S), wrap(z + dz, Z), wrap(y + dy, Y)
                    tc = wrap(c + dc, C)
                    arrived(grid.tile(tx, tz, ty, tc))
                    multiply(tx, tz, ty, tc)

                each(0, Z, other)
    states_out = pltpu.make_async_copy(held, states_ref, out_sem.at[1])
    states_out.start()
    for s in range(S):
        kv_ref[s * R : (s + 1) * R, :] = total[s].astype(jnp.bfloat16)

    each(1, Z, lambda dz: done(along_z(dz)))

    def sent(dz):
        done(spread(dz))
        for dx in range(1, S):
            done(pass_x(dx, dz))
        for dy in range(1, Y):
            done(pass_y(dy, dz))
        for dx in range(1, S):
            for dy in range(1, Y):
                t = grid.tile(wrap(x + dx, S), wrap(z + dz, Z), wrap(y + dy, Y), c)
                done(to_sibling(t, dx, dy, dz))

    each(0, Z, sent)
    weight_out.wait()
    states_out.wait()


def attention_kernel(len_ref, kv_ref, q_ref, g_ref, ctx_ref, qgrad_ref, kvgrad_ref):
    R = kv_ref.shape[0]
    T, L = q_ref.shape
    heads = L // HD
    limit = len_ref[pl.program_id(0)]
    q, g = q_ref[...], g_ref[...]
    keys, values = kv_ref[:, :L], kv_ref[:, L:]
    column = lax.broadcasted_iota(jnp.int32, (R, L), 1)
    pick = [
        jnp.where((column >= h * HD) & (column < (h + 1) * HD), 1.0, 0.0).astype(jnp.float32)
        for h in range(heads)
    ]
    key_stack = jnp.concatenate([keys * m.astype(jnp.bfloat16) for m in pick], axis=0)
    value_stack = jnp.concatenate([values * m.astype(jnp.bfloat16) for m in pick], axis=0)
    factor = HD ** (-0.5)
    f32 = jnp.float32
    scores = lax.dot_general(key_stack, q, NT, preferred_element_type=f32)
    prob_grad = lax.dot_general(value_stack, g, NT, preferred_element_type=f32)
    valid = lax.broadcasted_iota(jnp.int32, (R, T), 0) < limit
    probs, grads = [], []
    for h in range(heads):
        rows = slice(h * R, (h + 1) * R)
        score = jnp.where(valid, scores[rows] * factor, -1e30)
        exponent = jnp.exp(score - jnp.max(score, axis=0, keepdims=True))
        prob = exponent * (1.0 / jnp.sum(exponent, axis=0, keepdims=True))
        part = prob_grad[rows]
        mean = jnp.sum(part * prob, axis=0, keepdims=True)
        probs.append(prob.astype(jnp.bfloat16))
        grads.append((prob * (part - mean) * factor).astype(jnp.bfloat16))
    prob = jnp.concatenate(probs, axis=0)
    grad = jnp.concatenate(grads, axis=0)

    def own_columns(full):
        return sum(pick[h] * full[h * R : (h + 1) * R] for h in range(heads))

    value_grad = own_columns(jnp.dot(prob, g, preferred_element_type=f32))
    key_grad = own_columns(jnp.dot(grad, q, preferred_element_type=f32))
    kvgrad_ref[:, :L] = key_grad.astype(jnp.bfloat16)
    kvgrad_ref[:, L:] = value_grad.astype(jnp.bfloat16)
    ctx_ref[...] = lax.dot_general(prob, value_stack, TN, preferred_element_type=f32).astype(
        jnp.bfloat16
    )
    qgrad_ref[...] = lax.dot_general(grad, key_stack, TN, preferred_element_type=f32).astype(
        jnp.bfloat16
    )


def scatter_kernel(
    grid, kvgrad_ref, wcat_ref, out_ref,
    weight, mine, away, near, diag_a, diag_b, from_x, from_y, from_z, to_z,
    weight_sem, near_send, near_recv, a_send, a_recv, b_send, b_recv,
    x_send, x_recv, y_send, y_recv, z_send, z_recv,
):
    S, Y, Z, C = grid.S, grid.Y, grid.Z, grid.C
    R, F = out_ref.shape
    x, z, y, c = grid.here()
    bf16, f32 = jnp.bfloat16, jnp.float32
    weight_in = pltpu.make_async_copy(wcat_ref, weight, weight_sem.at[0])
    weight_in.start()
    grid.barrier()
    weight_in.wait()

    def term(tz, ty, tc):
        row = pl.multiple_of(grid.p(tz, ty, tc) * F, F)
        full = lax.dot_general(
            kvgrad_ref[...], weight[pl.ds(row, F), :], NT, preferred_element_type=f32
        )
        return full.reshape(S, R, F)

    def remote(src, dst, send, recv, target):
        return pltpu.make_async_remote_copy(
            src_ref=src, dst_ref=dst, send_sem=send, recv_sem=recv,
            device_id=target, device_id_type=MESH,
        )

    def near_copy(i):
        return remote(
            away.at[i], near.at[i], near_send.at[i], near_recv.at[i],
            grid.device(x, z, y, wrap(c + 1, C)),
        )

    def half_a(dx, dy, tz):
        i = ((dy - 1) * (S - 1) + dx - 1) * Z + tz
        ty = wrap(y + dy, Y)
        return remote(
            mine.at[tz * Y + ty, wrap(x + dx, S), pl.ds(0, R // 2)], diag_a.at[i],
            a_send.at[i], a_recv.at[i], grid.device(x, z, ty, c),
        )

    def half_b(dx, dy, tz):
        i = ((dy - 1) * (S - 1) + dx - 1) * Z + tz
        tx = wrap(x + dx, S)
        return remote(
            mine.at[tz * Y + wrap(y + dy, Y), tx, pl.ds(R // 2, R // 2)], diag_b.at[i],
            b_send.at[i], b_recv.at[i], grid.device(tx, z, y, c),
        )

    def along_x(dx, tz):
        i = (dx - 1) * Z + tz
        tx = wrap(x + dx, S)
        return remote(
            mine.at[tz * Y + y, tx], from_x.at[i], x_send.at[i], x_recv.at[i],
            grid.device(tx, z, y, c),
        )

    def along_y(dy, tz):
        i = (dy - 1) * Z + tz
        ty = wrap(y + dy, Y)
        return remote(
            mine.at[tz * Y + ty, x], from_y.at[i], y_send.at[i], y_recv.at[i],
            grid.device(x, z, ty, c),
        )

    def along_z(dz):
        tz = wrap(z + dz, Z)
        return remote(
            to_z.at[dz], from_z.at[dz], z_send.at[dz], z_recv.at[dz],
            grid.device(x, tz, y, c),
        )

    if C > 1:
        for dy in [*range(1, Y), 0]:

            def give(dz):
                tz, ty = wrap(z + dz, Z), wrap(y + dy, Y)
                i = tz * Y + ty
                away[i] = term(tz, ty, wrap(c + 1, C)).astype(bf16)
                near_copy(i).start()

            each(1, Z + 1, give)

    def collect(dz, dy):
        tz, ty = wrap(z + dz, Z), wrap(y + dy, Y)
        i = tz * Y + ty
        value = term(tz, ty, c)
        if C > 1:
            near_copy(i).wait_recv()
            value = value + near[i].astype(f32)
        mine[i] = value.astype(bf16)
        if dy:
            for dx in range(1, S):
                half_a(dx, dy, tz).start()
                half_b(dx, dy, tz).start()

    for dy in [*range(1, Y), 0]:
        each(1, Z + 1, lambda dz: collect(dz, dy))

    def sides(dz):
        tz = wrap(z + dz, Z)
        for dx in range(1, S):
            tx = wrap(x + dx, S)
            for dy in range(1, Y):
                copy = half_a(dx, dy, tz)
                copy.wait_recv()
                i = ((dy - 1) * (S - 1) + dx - 1) * Z + tz
                spot = (tz * Y + y, tx, pl.ds(0, R // 2))
                mine[spot] = (mine[spot].astype(f32) + diag_a[i].astype(f32)).astype(bf16)
            along_x(dx, tz).start()
        for dy in range(1, Y):
            ty = wrap(y + dy, Y)
            for dx in range(1, S):
                half_b(dx, dy, tz).wait_recv()
                i = ((dy - 1) * (S - 1) + dx - 1) * Z + tz
                spot = (tz * Y + ty, x, pl.ds(R // 2, R // 2))
                mine[spot] = (mine[spot].astype(f32) + diag_b[i].astype(f32)).astype(bf16)
            along_y(dy, tz).start()

    each(1, Z + 1, sides)

    def joined(dz):
        tz = wrap(z + dz, Z)
        value = mine[tz * Y + y, x].astype(f32)
        for dx in range(1, S):
            along_x(dx, tz).wait_recv()
            value = value + from_x[(dx - 1) * Z + tz].astype(f32)
        for dy in range(1, Y):
            along_y(dy, tz).wait_recv()
            value = value + from_y[(dy - 1) * Z + tz].astype(f32)
        return value

    def pass_on(dz):
        to_z[dz] = joined(dz).astype(bf16)
        along_z(dz).start()

    each(1, Z, pass_on)
    value = joined(0)
    for dz in range(1, Z):
        along_z(dz).wait_recv()
        value = value + from_z[dz].astype(f32)
    out_ref[...] = value.astype(bf16)

    def sent(tz):
        for dy in range(Y):
            if C > 1:
                near_copy(tz * Y + dy).wait_send()
        for dx in range(1, S):
            along_x(dx, tz).wait_send()
            for dy in range(1, Y):
                half_a(dx, dy, tz).wait_send()
                half_b(dx, dy, tz).wait_send()
        for dy in range(1, Y):
            along_y(dy, tz).wait_send()

    each(0, Z, sent)
    each(1, Z, lambda dz: along_z(dz).wait_send())


def weight_grad_kernel(sections, states_ref, kvgrad_ref, out_ref, packed, wide, sem):
    M, lane_tiles = packed.shape[:2]
    R, F = states_ref.shape[1:]
    L = kvgrad_ref.shape[1] // 2

    def put(p, j):
        return pltpu.make_async_copy(
            packed.at[p, j],
            out_ref.at[pl.ds(pl.multiple_of(p * F, F), F), :, pl.ds(j * LANES, LANES)],
            sem.at[p, j],
        )

    def block(p):
        states = jnp.concatenate([states_ref[s * M + p] for s in range(sections)], axis=0)
        full = lax.dot_general(states, kvgrad_ref[...], TN, preferred_element_type=jnp.float32)
        for j in range(lane_tiles):
            for kind in range(2):
                first = kind * L + j * LANES
                wide[j, pl.ds(kind, F, stride=2), :] = full[:, first : first + LANES]
            packed.at[p, j].reshape(2 * F, LANES)[...] = wide[j].astype(jnp.bfloat16)
            put(p, j).start()

    each(0, M, block)

    def finish(p):
        for j in range(lane_tiles):
            put(p, j).wait()

    each(0, M, finish)


def shards(grid, enc_final, enc_len, kv_weight, queries, d_context):
    S, M, C, Y, Z = grid.S, grid.M, grid.C, grid.Y, grid.Z
    R, F = enc_final.shape[1:]
    D, _, L = kv_weight.shape[1:]
    T = queries.shape[2]
    lane_tiles = L // LANES
    bf16, f32 = jnp.bfloat16, jnp.float32
    dma = pltpu.SemaphoreType.DMA
    vmem = pl.BlockSpec(memory_space=pltpu.VMEM)
    anywhere = pl.BlockSpec(memory_space=pl.ANY)
    shape = jax.ShapeDtypeStruct
    sends = Z + (S - 1) * Z + (Y - 1) * Z + 2 * (S - 1) * (Y - 1) * Z + S * Y * Z
    states, wcat, key_value = pl.pallas_call(
        functools.partial(gather_kernel, grid),
        out_shape=(
            shape((S * M, R, F), bf16), shape((D, 2 * L), bf16), shape((S * R, 2 * L), bf16),
        ),
        in_specs=[vmem, anywhere],
        out_specs=(anywhere, anywhere, vmem),
        scratch_shapes=[
            pltpu.VMEM((S * M, R, F), bf16),
            pltpu.VMEM((D, 2 * L), bf16),
            pltpu.VMEM((lane_tiles, D, 2, LANES), bf16),
            pltpu.VMEM((2 * F, LANES), f32),
            pltpu.VMEM((S, R, 2 * L), f32),
            dma((lane_tiles,)),
            dma((sends,)),
            dma((2, S * M)),
            dma((2,)),
        ],
        compiler_params=pltpu.CompilerParams(
            collective_id=0, has_side_effects=True, vmem_limit_bytes=VMEM_BYTES
        ),
        name="gather_states",
    )(enc_final[0], kv_weight[0])

    rows = pl.BlockSpec((R, 2 * L), lambda m: (m, 0))
    long = pl.BlockSpec((None, T, L), lambda m: (m, 0, 0))
    context, query_grad, kv_grad = pl.pallas_call(
        attention_kernel,
        grid=(S,),
        out_shape=(
            shape((S, T, L), bf16), shape((S, T, L), bf16), shape((S * R, 2 * L), bf16),
        ),
        in_specs=[pl.BlockSpec(memory_space=pltpu.SMEM), rows, long, long],
        out_specs=(long, long, rows),
        compiler_params=pltpu.CompilerParams(vmem_limit_bytes=VMEM_BYTES),
        name="attention",
    )(enc_len, key_value, queries[0], d_context[0])

    pair = max((S - 1) * (Y - 1) * Z, 1)
    enc_grad = pl.pallas_call(
        functools.partial(scatter_kernel, grid),
        out_shape=shape((R, F), bf16),
        in_specs=[vmem, anywhere],
        out_specs=vmem,
        scratch_shapes=[
            pltpu.VMEM((D, 2 * L), bf16),
            pltpu.VMEM((Z * Y, S, R, F), bf16),
            pltpu.VMEM((Z * Y, S, R, F), bf16),
            pltpu.VMEM((Z * Y, S, R, F), bf16),
            pltpu.VMEM((pair, R // 2, F), bf16),
            pltpu.VMEM((pair, R // 2, F), bf16),
            pltpu.VMEM((max(S - 1, 1) * Z, R, F), bf16),
            pltpu.VMEM((max(Y - 1, 1) * Z, R, F), bf16),
            pltpu.VMEM((Z, R, F), bf16),
            pltpu.VMEM((Z, R, F), bf16),
            dma((1,)),
            dma((Z * Y,)), dma((Z * Y,)),
            dma((pair,)), dma((pair,)), dma((pair,)), dma((pair,)),
            dma((max(S - 1, 1) * Z,)), dma((max(S - 1, 1) * Z,)),
            dma((max(Y - 1, 1) * Z,)), dma((max(Y - 1, 1) * Z,)),
            dma((Z,)), dma((Z,)),
        ],
        compiler_params=pltpu.CompilerParams(
            collective_id=1, has_side_effects=True, vmem_limit_bytes=VMEM_BYTES
        ),
        name="scatter_states_grad",
    )(kv_grad, wcat)

    weight_grad = pl.pallas_call(
        functools.partial(weight_grad_kernel, S),
        out_shape=shape((D, 2, L), bf16),
        in_specs=[vmem, vmem],
        out_specs=anywhere,
        scratch_shapes=[
            pltpu.VMEM((M, lane_tiles, F, 2, LANES), bf16),
            pltpu.VMEM((lane_tiles, 2 * F, LANES), f32),
            dma((M, lane_tiles)),
        ],
        compiler_params=pltpu.CompilerParams(vmem_limit_bytes=VMEM_BYTES),
        name="weight_grad",
    )(states, kv_grad)
    return context[None], query_grad[None], weight_grad[None], enc_grad[None]


def solution(mesh):
    grid = Grid(mesh.shape["section"], mesh.shape["mp"])
    split = P("section", None, None, "mp")
    return jax.shard_map(
        functools.partial(shards, grid),
        mesh=mesh,
        in_specs=(P("section", None, "mp"), P(), split, split, split),
        out_specs=(split, split, split, P("section", None, "mp")),
        check_vma=False,
    )
```

```python
import functools

import jax
import jax.numpy as jnp
from jax import lax
from jax.experimental import pallas as pl
from jax.experimental.pallas import tpu as pltpu
from jax.sharding import PartitionSpec as P

HD = 64
LANES = 128
MESH = pl.DeviceIdType.MESH
VMEM_BYTES = 56 * 2**20
UNROLL = 4
NT = (((1,), (1,)), ((), ()))
TN = (((0,), (0,)), ((), ()))


def wrap(value, size):
    return lax.rem(value, size)


class Grid:
    def __init__(self, section, mp):
        self.S, self.M = section, mp
        self.C = 2 if mp % 2 == 0 else 1
        self.Y = 2 if (mp // self.C) % 2 == 0 else 1
        self.Z = mp // self.C // self.Y

    def here(self):
        x, p = lax.axis_index("section"), lax.axis_index("mp")
        c = lax.rem(p, self.C)
        zy = lax.div(p, self.C)
        return x, lax.div(zy, self.Y), lax.rem(zy, self.Y), c

    def p(self, z, y, c):
        return (z * self.Y + y) * self.C + c

    def tile(self, x, z, y, c):
        return x, self.p(z, y, c)

    def device(self, x, z, y, c):
        return (x, self.p(z, y, c))

    def barrier(self):
        x, z, y, c = self.here()
        sem = pltpu.get_barrier_semaphore()
        peers = [self.device(wrap(x + d, self.S), z, y, c) for d in range(1, self.S)]
        peers += [self.device(x, wrap(z + d, self.Z), y, c) for d in range(1, self.Z)]
        peers += [self.device(x, z, wrap(y + d, self.Y), c) for d in range(1, self.Y)]
        peers += [self.device(x, z, y, wrap(c + d, self.C)) for d in range(1, self.C)]
        for peer in peers:
            pl.semaphore_signal(sem, inc=1, device_id=peer, device_id_type=MESH)
        pl.semaphore_wait(sem, len(peers))


def each(low, high, body):
    def step(i, carry):
        body(i)
        return carry

    lax.fori_loop(low, high, step, 0)


def select(back):
    across = lax.broadcasted_iota(jnp.int32, (2 * LANES, 2 * LANES), 1 - back)
    along = lax.broadcasted_iota(jnp.int32, (2 * LANES, 2 * LANES), back)
    source = jnp.where(along < LANES, 2 * along, 2 * (along - LANES) + 1)
    return jnp.where(across == source, 1.0, 0.0).astype(jnp.float32).astype(jnp.bfloat16)


def gather_kernel(
    grid, enc_ref, w_ref, states_ref, wcat_ref, kv_ref,
    held, weight, raw, pick, total, raw_sem, send_sem, recv_sem, out_sem,
):
    S, Y, Z, C = grid.S, grid.Y, grid.Z, grid.C
    R, F = enc_ref.shape
    depth = weight.shape[0]
    L = weight.shape[1] // 2
    lane_tiles = L // LANES
    x, z, y, c = grid.here()

    def fetch(j):
        return pltpu.make_async_copy(
            w_ref.at[:, :, pl.ds(j * LANES, LANES)], raw.at[j], raw_sem.at[j]
        )

    for j in range(lane_tiles):
        fetch(j).start()
    held[grid.tile(x, z, y, c)] = enc_ref[...]
    total[...] = jnp.zeros_like(total)
    grid.barrier()

    whole = pl.ds(0, R)
    upper, lower = pl.ds(0, R // 2), pl.ds(R // 2, R // 2)
    at_x = Z
    at_y = at_x + (S - 1) * Z
    at_a = at_y + (Y - 1) * Z
    at_b = at_a + (S - 1) * (Y - 1) * Z
    at_s = at_b + (S - 1) * (Y - 1) * Z

    def move(t, rows, target, slot, part=0):
        return pltpu.make_async_remote_copy(
            src_ref=held.at[(*t, rows)],
            dst_ref=held.at[(*t, rows)],
            send_sem=send_sem.at[slot],
            recv_sem=recv_sem.at[(part, *t)],
            device_id=target,
            device_id_type=MESH,
        )

    def arrived(t, rows=whole, part=0):
        move(t, rows, grid.device(wrap(x + 1, S), z, y, c), 0, part).wait_recv()

    def to_sibling(t, dx, dy, dz):
        return [
            move(t, whole, grid.device(x, z, y, wrap(c + d, C)), at_s + (dx * Y + dy) * Z + dz)
            for d in range(1, C)
        ]

    def spread(dz):
        t = grid.tile(x, wrap(z + dz, Z), y, c)
        copies = [
            move(t, whole, grid.device(wrap(x + d, S), z, y, c), at_x + (d - 1) * Z + dz)
            for d in range(1, S)
        ]
        copies += [
            move(t, whole, grid.device(x, z, wrap(y + d, Y), c), at_y + (d - 1) * Z + dz)
            for d in range(1, Y)
        ]
        return copies + to_sibling(t, 0, 0, dz)

    def pass_x(dx, dz):
        t = grid.tile(wrap(x + dx, S), wrap(z + dz, Z), y, c)
        copies = [
            move(t, upper, grid.device(x, z, wrap(y + d, Y), c),
                 at_a + ((dx - 1) * (Y - 1) + d - 1) * Z + dz, 0)
            for d in range(1, Y)
        ]
        return copies + to_sibling(t, dx, 0, dz)

    def pass_y(dy, dz):
        t = grid.tile(x, wrap(z + dz, Z), wrap(y + dy, Y), c)
        copies = [
            move(t, lower, grid.device(wrap(x + d, S), z, y, c),
                 at_b + ((d - 1) * (Y - 1) + dy - 1) * Z + dz, 1)
            for d in range(1, S)
        ]
        return copies + to_sibling(t, 0, dy, dz)

    def start(copies):
        for copy in copies:
            copy.start()

    def done(copies):
        for copy in copies:
            copy.wait_send()

    own = grid.tile(x, z, y, c)

    def along_z(dz):
        return [move(own, whole, grid.device(x, wrap(z + dz, Z), y, c), dz)]

    each(1, Z, lambda dz: start(along_z(dz)))
    start(spread(0))

    def unpack(low, high):
        def block(i):
            for u in range(UNROLL):
                group = i * UNROLL + u
                both = jnp.concatenate(
                    [
                        raw.at[j].reshape(2 * depth, LANES)[
                            pl.ds(pl.multiple_of(group * 2 * LANES, 2 * LANES), 2 * LANES), :
                        ]
                        for j in range(lane_tiles)
                    ],
                    axis=1,
                )
                apart = jnp.dot(pick[...], both, preferred_element_type=jnp.float32).astype(
                    jnp.bfloat16
                )
                row = pl.ds(pl.multiple_of(group * LANES, LANES), LANES)
                weight[row, :L] = apart[:LANES]
                weight[row, L:] = apart[LANES:]

        each(low, high, block)

    blocks = depth // (LANES * UNROLL)
    pick[...] = select(0)
    for j in range(lane_tiles):
        fetch(j).wait()
    unpack(0, blocks // 2)

    def column(dz):
        arrived(grid.tile(x, wrap(z + dz, Z), y, c))
        start(spread(dz))

    each(1, Z, column)
    unpack(blocks // 2, blocks)
    weight_out = pltpu.make_async_copy(weight, wcat_ref, out_sem.at[0])
    weight_out.start()

    def multiply(tz, ty, tc):
        p = grid.p(tz, ty, tc)
        total[...] += jnp.dot(
            held[:, p].reshape(S * R, F),
            weight[pl.ds(pl.multiple_of(p * F, F), F), :],
            preferred_element_type=jnp.float32,
        )

    def sides(dz):
        tz = wrap(z + dz, Z)
        for dx in range(1, S):
            arrived(grid.tile(wrap(x + dx, S), tz, y, c))
            start(pass_x(dx, dz))
        for dy in range(1, Y):
            arrived(grid.tile(x, tz, wrap(y + dy, Y), c))
            start(pass_y(dy, dz))
        multiply(tz, y, c)

    each(0, Z, sides)

    def diagonal(dz):
        tz = wrap(z + dz, Z)
        for dy in range(1, Y):
            ty = wrap(y + dy, Y)
            for dx in range(1, S):
                t = grid.tile(wrap(x + dx, S), tz, ty, c)
                arrived(t, upper, 0)
                arrived(t, lower, 1)
                start(to_sibling(t, dx, dy, dz))
            multiply(tz, ty, c)

    each(0, Z, diagonal)

    for dc in range(1, C):
        for dy in range(Y):

            def other(dz):
                tz, ty, tc = wrap(z + dz, Z), wrap(y + dy, Y), wrap(c + dc, C)
                for dx in range(S):
                    arrived(grid.tile(wrap(x + dx, S), tz, ty, tc))
                multiply(tz, ty, tc)

            each(0, Z, other)
    states_out = pltpu.make_async_copy(held, states_ref, out_sem.at[1])
    states_out.start()
    kv_ref[...] = total[...].astype(jnp.bfloat16)

    each(1, Z, lambda dz: done(along_z(dz)))

    def sent(dz):
        done(spread(dz))
        for dx in range(1, S):
            done(pass_x(dx, dz))
        for dy in range(1, Y):
            done(pass_y(dy, dz))
        for dx in range(1, S):
            for dy in range(1, Y):
                t = grid.tile(wrap(x + dx, S), wrap(z + dz, Z), wrap(y + dy, Y), c)
                done(to_sibling(t, dx, dy, dz))

    each(0, Z, sent)
    weight_out.wait()
    states_out.wait()


def attention_kernel(len_ref, kv_ref, q_ref, g_ref, ctx_ref, qgrad_ref, kvgrad_ref):
    R = kv_ref.shape[0]
    T, L = q_ref.shape
    heads = L // HD
    limit = len_ref[pl.program_id(0)]
    q, g = q_ref[...], g_ref[...]
    keys, values = kv_ref[:, :L], kv_ref[:, L:]
    column = lax.broadcasted_iota(jnp.int32, (R, L), 1)
    pick = [
        jnp.where((column >= h * HD) & (column < (h + 1) * HD), 1.0, 0.0).astype(jnp.float32)
        for h in range(heads)
    ]
    key_stack = jnp.concatenate([keys * m.astype(jnp.bfloat16) for m in pick], axis=0)
    value_stack = jnp.concatenate([values * m.astype(jnp.bfloat16) for m in pick], axis=0)
    factor = HD ** (-0.5)
    f32 = jnp.float32
    scores = lax.dot_general(key_stack, q, NT, preferred_element_type=f32)
    prob_grad = lax.dot_general(value_stack, g, NT, preferred_element_type=f32)
    valid = lax.broadcasted_iota(jnp.int32, (R, T), 0) < limit
    probs, grads = [], []
    for h in range(heads):
        rows = slice(h * R, (h + 1) * R)
        score = jnp.where(valid, scores[rows] * factor, -1e30)
        exponent = jnp.exp(score - jnp.max(score, axis=0, keepdims=True))
        prob = exponent * (1.0 / jnp.sum(exponent, axis=0, keepdims=True))
        part = prob_grad[rows]
        mean = jnp.sum(part * prob, axis=0, keepdims=True)
        probs.append(prob.astype(jnp.bfloat16))
        grads.append((prob * (part - mean) * factor).astype(jnp.bfloat16))
    prob = jnp.concatenate(probs, axis=0)
    grad = jnp.concatenate(grads, axis=0)

    def own_columns(full):
        return sum(pick[h] * full[h * R : (h + 1) * R] for h in range(heads))

    value_grad = own_columns(jnp.dot(prob, g, preferred_element_type=f32))
    key_grad = own_columns(jnp.dot(grad, q, preferred_element_type=f32))
    kvgrad_ref[:, :L] = key_grad.astype(jnp.bfloat16)
    kvgrad_ref[:, L:] = value_grad.astype(jnp.bfloat16)
    ctx_ref[...] = lax.dot_general(prob, value_stack, TN, preferred_element_type=f32).astype(
        jnp.bfloat16
    )
    qgrad_ref[...] = lax.dot_general(grad, key_stack, TN, preferred_element_type=f32).astype(
        jnp.bfloat16
    )


def scatter_kernel(
    grid, kvgrad_ref, wcat_ref, states_ref, out_ref, wgrad_ref,
    weight, states, packed, pick, mine, away, near, diag_a, diag_b, from_x, from_y, from_z, to_z,
    weight_sem, near_send, near_recv, a_send, a_recv, b_send, b_recv,
    x_send, x_recv, y_send, y_recv, z_send, z_recv, packed_sem,
):
    S, Y, Z, C = grid.S, grid.Y, grid.Z, grid.C
    R, F = out_ref.shape
    x, z, y, c = grid.here()
    bf16, f32 = jnp.bfloat16, jnp.float32
    weight_in = pltpu.make_async_copy(wcat_ref, weight, weight_sem.at[0])
    weight_in.start()
    states_in = pltpu.make_async_copy(states_ref, states, weight_sem.at[1])
    states_in.start()
    pick[...] = select(1)
    grid.barrier()
    weight_in.wait()

    def term(tz, ty, tc):
        row = pl.multiple_of(grid.p(tz, ty, tc) * F, F)
        full = lax.dot_general(
            kvgrad_ref[...], weight[pl.ds(row, F), :], NT, preferred_element_type=f32
        )
        return full.reshape(S, R, F)

    M, lane_tiles = packed.shape[:2]
    L = lane_tiles * LANES

    def put(p, j):
        return pltpu.make_async_copy(
            packed.at[p, j],
            wgrad_ref.at[pl.ds(pl.multiple_of(p * F, F), F), :, pl.ds(j * LANES, LANES)],
            packed_sem.at[p, j],
        )

    def weight_block(p):
        full = lax.dot_general(
            states[:, p].reshape(S * R, F), kvgrad_ref[...], TN, preferred_element_type=f32
        ).astype(bf16)
        for g in range(F // LANES):
            rows = full[g * LANES : (g + 1) * LANES]
            both = jnp.concatenate([rows[:, :L], rows[:, L:]], axis=0)
            mixed = jnp.dot(pick[...], both, preferred_element_type=f32).astype(bf16)
            for j in range(lane_tiles):
                packed.at[p, j].reshape(2 * F, LANES)[
                    g * 2 * LANES : (g + 1) * 2 * LANES, :
                ] = mixed[:, j * LANES : (j + 1) * LANES]
        for j in range(lane_tiles):
            put(p, j).start()

    def remote(src, dst, send, recv, target):
        return pltpu.make_async_remote_copy(
            src_ref=src, dst_ref=dst, send_sem=send, recv_sem=recv,
            device_id=target, device_id_type=MESH,
        )

    def near_copy(i):
        return remote(
            away.at[i], near.at[i], near_send.at[i], near_recv.at[i],
            grid.device(x, z, y, wrap(c + 1, C)),
        )

    def half_a(dx, dy, tz):
        i = ((dy - 1) * (S - 1) + dx - 1) * Z + tz
        ty = wrap(y + dy, Y)
        return remote(
            mine.at[tz * Y + ty, wrap(x + dx, S), pl.ds(0, R // 2)], diag_a.at[i],
            a_send.at[i], a_recv.at[i], grid.device(x, z, ty, c),
        )

    def half_b(dx, dy, tz):
        i = ((dy - 1) * (S - 1) + dx - 1) * Z + tz
        tx = wrap(x + dx, S)
        return remote(
            mine.at[tz * Y + wrap(y + dy, Y), tx, pl.ds(R // 2, R // 2)], diag_b.at[i],
            b_send.at[i], b_recv.at[i], grid.device(tx, z, y, c),
        )

    def along_x(dx, tz):
        i = (dx - 1) * Z + tz
        tx = wrap(x + dx, S)
        return remote(
            mine.at[tz * Y + y, tx], from_x.at[i], x_send.at[i], x_recv.at[i],
            grid.device(tx, z, y, c),
        )

    def along_y(dy, tz):
        i = (dy - 1) * Z + tz
        ty = wrap(y + dy, Y)
        return remote(
            mine.at[tz * Y + ty, x], from_y.at[i], y_send.at[i], y_recv.at[i],
            grid.device(x, z, ty, c),
        )

    def along_z(dz):
        tz = wrap(z + dz, Z)
        return remote(
            to_z.at[dz], from_z.at[dz], z_send.at[dz], z_recv.at[dz],
            grid.device(x, tz, y, c),
        )

    if C > 1:
        for dy in [*range(1, Y), 0]:

            def give(dz):
                tz, ty = wrap(z + dz, Z), wrap(y + dy, Y)
                i = tz * Y + ty
                away[i] = term(tz, ty, wrap(c + 1, C)).astype(bf16)
                near_copy(i).start()

            each(1, Z + 1, give)

    def collect(dz, dy):
        tz, ty = wrap(z + dz, Z), wrap(y + dy, Y)
        i = tz * Y + ty
        value = term(tz, ty, c)
        if C > 1:
            near_copy(i).wait_recv()
            value = value + near[i].astype(f32)
        mine[i] = value.astype(bf16)
        if dy:
            for dx in range(1, S):
                half_a(dx, dy, tz).start()
                half_b(dx, dy, tz).start()

    for dy in [*range(1, Y), 0]:
        each(1, Z + 1, lambda dz: collect(dz, dy))

    states_in.wait()
    first, second = 3 * M // 16, 10 * M // 16
    each(0, first, weight_block)

    def sides(dz):
        tz = wrap(z + dz, Z)
        for dx in range(1, S):
            tx = wrap(x + dx, S)
            for dy in range(1, Y):
                copy = half_a(dx, dy, tz)
                copy.wait_recv()
                i = ((dy - 1) * (S - 1) + dx - 1) * Z + tz
                spot = (tz * Y + y, tx, pl.ds(0, R // 2))
                mine[spot] = (mine[spot].astype(f32) + diag_a[i].astype(f32)).astype(bf16)
            along_x(dx, tz).start()
        for dy in range(1, Y):
            ty = wrap(y + dy, Y)
            for dx in range(1, S):
                half_b(dx, dy, tz).wait_recv()
                i = ((dy - 1) * (S - 1) + dx - 1) * Z + tz
                spot = (tz * Y + ty, x, pl.ds(R // 2, R // 2))
                mine[spot] = (mine[spot].astype(f32) + diag_b[i].astype(f32)).astype(bf16)
            along_y(dy, tz).start()

    each(1, Z + 1, sides)
    each(first, second, weight_block)

    def joined(dz):
        tz = wrap(z + dz, Z)
        value = mine[tz * Y + y, x].astype(f32)
        for dx in range(1, S):
            along_x(dx, tz).wait_recv()
            value = value + from_x[(dx - 1) * Z + tz].astype(f32)
        for dy in range(1, Y):
            along_y(dy, tz).wait_recv()
            value = value + from_y[(dy - 1) * Z + tz].astype(f32)
        return value

    def pass_on(dz):
        to_z[dz] = joined(dz).astype(bf16)
        along_z(dz).start()

    each(1, Z, pass_on)
    each(second, M, weight_block)
    value = joined(0)
    for dz in range(1, Z):
        along_z(dz).wait_recv()
        value = value + from_z[dz].astype(f32)
    out_ref[...] = value.astype(bf16)

    def sent(tz):
        for dy in range(Y):
            if C > 1:
                near_copy(tz * Y + dy).wait_send()
        for dx in range(1, S):
            along_x(dx, tz).wait_send()
            for dy in range(1, Y):
                half_a(dx, dy, tz).wait_send()
                half_b(dx, dy, tz).wait_send()
        for dy in range(1, Y):
            along_y(dy, tz).wait_send()

    each(0, Z, sent)
    each(1, Z, lambda dz: along_z(dz).wait_send())

    def written(p):
        for j in range(lane_tiles):
            put(p, j).wait()

    each(0, M, written)


def settle_kernel(from_ref, to_ref, sem):
    count = sem.shape[0]
    rows = from_ref.shape[0] // count
    copies = [
        pltpu.make_async_copy(
            from_ref.at[pl.ds(i * rows, rows)], to_ref.at[pl.ds(i * rows, rows)], sem.at[i]
        )
        for i in range(count)
    ]
    for copy in copies:
        copy.start()
    for copy in copies:
        copy.wait()


def shards(grid, enc_final, enc_len, kv_weight, queries, d_context):
    S, M, C, Y, Z = grid.S, grid.M, grid.C, grid.Y, grid.Z
    R, F = enc_final.shape[1:]
    D, _, L = kv_weight.shape[1:]
    T = queries.shape[2]
    lane_tiles = L // LANES
    bf16, f32 = jnp.bfloat16, jnp.float32
    dma = pltpu.SemaphoreType.DMA
    vmem = pl.BlockSpec(memory_space=pltpu.VMEM)
    anywhere = pl.BlockSpec(memory_space=pl.ANY)
    shape = jax.ShapeDtypeStruct
    sends = Z + (S - 1) * Z + (Y - 1) * Z + 2 * (S - 1) * (Y - 1) * Z + S * Y * Z
    states, wcat, key_value = pl.pallas_call(
        functools.partial(gather_kernel, grid),
        out_shape=(
            shape((S, M, R, F), bf16), shape((D, 2 * L), bf16), shape((S * R, 2 * L), bf16),
        ),
        in_specs=[vmem, anywhere],
        out_specs=(anywhere, anywhere, vmem),
        scratch_shapes=[
            pltpu.VMEM((S, M, R, F), bf16),
            pltpu.VMEM((D, 2 * L), bf16),
            pltpu.VMEM((lane_tiles, D, 2, LANES), bf16),
            pltpu.VMEM((2 * LANES, 2 * LANES), bf16),
            pltpu.VMEM((S * R, 2 * L), f32),
            dma((lane_tiles,)),
            dma((sends,)),
            dma((2, S, M)),
            dma((2,)),
        ],
        compiler_params=pltpu.CompilerParams(
            collective_id=0, has_side_effects=True, vmem_limit_bytes=VMEM_BYTES
        ),
        name="gather_states",
    )(enc_final[0], kv_weight[0])

    rows = pl.BlockSpec((R, 2 * L), lambda m: (m, 0))
    long = pl.BlockSpec((None, T, L), lambda m: (m, 0, 0))
    context, query_grad, kv_grad = pl.pallas_call(
        attention_kernel,
        grid=(S,),
        out_shape=(
            shape((S, T, L), bf16), shape((S, T, L), bf16), shape((S * R, 2 * L), bf16),
        ),
        in_specs=[pl.BlockSpec(memory_space=pltpu.SMEM), rows, long, long],
        out_specs=(long, long, rows),
        compiler_params=pltpu.CompilerParams(vmem_limit_bytes=VMEM_BYTES),
        name="attention",
    )(enc_len, key_value, queries[0], d_context[0])

    pair = max((S - 1) * (Y - 1) * Z, 1)
    enc_grad, weight_grad = pl.pallas_call(
        functools.partial(scatter_kernel, grid),
        out_shape=(shape((R, F), bf16), shape((D, 2, L), bf16)),
        in_specs=[vmem, anywhere, anywhere],
        out_specs=(vmem, anywhere),
        scratch_shapes=[
            pltpu.VMEM((D, 2 * L), bf16),
            pltpu.VMEM((S, M, R, F), bf16),
            pltpu.VMEM((M, lane_tiles, F, 2, LANES), bf16),
            pltpu.VMEM((2 * LANES, 2 * LANES), bf16),
            pltpu.VMEM((Z * Y, S, R, F), bf16),
            pltpu.VMEM((Z * Y, S, R, F), bf16),
            pltpu.VMEM((Z * Y, S, R, F), bf16),
            pltpu.VMEM((pair, R // 2, F), bf16),
            pltpu.VMEM((pair, R // 2, F), bf16),
            pltpu.VMEM((max(S - 1, 1) * Z, R, F), bf16),
            pltpu.VMEM((max(Y - 1, 1) * Z, R, F), bf16),
            pltpu.VMEM((Z, R, F), bf16),
            pltpu.VMEM((Z, R, F), bf16),
            dma((2,)),
            dma((Z * Y,)), dma((Z * Y,)),
            dma((pair,)), dma((pair,)), dma((pair,)), dma((pair,)),
            dma((max(S - 1, 1) * Z,)), dma((max(S - 1, 1) * Z,)),
            dma((max(Y - 1, 1) * Z,)), dma((max(Y - 1, 1) * Z,)),
            dma((Z,)), dma((Z,)), dma((M, lane_tiles)),
        ],
        compiler_params=pltpu.CompilerParams(
            collective_id=1, has_side_effects=True, vmem_limit_bytes=VMEM_BYTES
        ),
        name="scatter_states_grad",
    )(kv_grad, wcat, states)

    weight_grad = pl.pallas_call(
        settle_kernel,
        out_shape=shape((D, 2, L), bf16),
        in_specs=[anywhere],
        out_specs=anywhere,
        scratch_shapes=[dma((8,))],
        name="settle_weight_grad",
    )(weight_grad)
    return context[None], query_grad[None], weight_grad[None], enc_grad[None]


def solution(mesh):
    grid = Grid(mesh.shape["section"], mesh.shape["mp"])
    split = P("section", None, None, "mp")
    return jax.shard_map(
        functools.partial(shards, grid),
        mesh=mesh,
        in_specs=(P("section", None, "mp"), P(), split, split, split),
        out_specs=(split, split, split, P("section", None, "mp")),
        check_vma=False,
    )
```

```python
import functools

import jax
import jax.numpy as jnp
from jax import lax
from jax.experimental import pallas as pl
from jax.experimental.pallas import tpu as pltpu
from jax.sharding import PartitionSpec as P

HD = 64
LANES = 128
MESH = pl.DeviceIdType.MESH
VMEM_BYTES = 56 * 2**20
UNROLL = 4
NT = (((1,), (1,)), ((), ()))
TN = (((0,), (0,)), ((), ()))


def wrap(value, size):
    return lax.rem(value, size)


class Grid:
    def __init__(self, section, mp):
        self.S, self.M = section, mp
        self.C = 2 if mp % 2 == 0 else 1
        self.Y = 2 if (mp // self.C) % 2 == 0 else 1
        self.Z = mp // self.C // self.Y

    def here(self):
        x, p = lax.axis_index("section"), lax.axis_index("mp")
        c = lax.rem(p, self.C)
        zy = lax.div(p, self.C)
        return x, lax.div(zy, self.Y), lax.rem(zy, self.Y), c

    def p(self, z, y, c):
        return (z * self.Y + y) * self.C + c

    def tile(self, x, z, y, c):
        return x, self.p(z, y, c)

    def device(self, x, z, y, c):
        return (x, self.p(z, y, c))

    def barrier(self):
        x, z, y, c = self.here()
        sem = pltpu.get_barrier_semaphore()
        peers = [self.device(wrap(x + d, self.S), z, y, c) for d in range(1, self.S)]
        peers += [self.device(x, wrap(z + d, self.Z), y, c) for d in range(1, self.Z)]
        peers += [self.device(x, z, wrap(y + d, self.Y), c) for d in range(1, self.Y)]
        peers += [self.device(x, z, y, wrap(c + d, self.C)) for d in range(1, self.C)]
        for peer in peers:
            pl.semaphore_signal(sem, inc=1, device_id=peer, device_id_type=MESH)
        pl.semaphore_wait(sem, len(peers))


def each(low, high, body):
    def step(i, carry):
        body(i)
        return carry

    lax.fori_loop(low, high, step, 0)


def select(lane_tiles, back):
    size = 2 * LANES
    count = size // (2 * lane_tiles)
    across = lax.broadcasted_iota(jnp.int32, (size, size), 1 - back)
    along = lax.broadcasted_iota(jnp.int32, (size, size), back)
    hit = jnp.zeros((size, size), jnp.float32)
    for kind in range(2):
        for j in range(lane_tiles):
            low = (kind * lane_tiles + j) * count
            source = (along - low) * (2 * lane_tiles) + 2 * j + kind
            inside = (along >= low) & (along < low + count)
            hit = jnp.where(inside & (across == source), 1.0, hit)
    return hit.astype(jnp.bfloat16)


def gather_kernel(
    grid, enc_ref, w_ref, states_ref, wcat_ref, kv_ref,
    held, weight, raw, pick, total, raw_sem, send_sem, recv_sem, out_sem,
):
    S, Y, Z, C = grid.S, grid.Y, grid.Z, grid.C
    R, F = enc_ref.shape
    depth = weight.shape[0]
    L = weight.shape[1] // 2
    lane_tiles = L // LANES
    x, z, y, c = grid.here()

    parts = raw_sem.shape[0]
    part_rows = raw.shape[0] // parts

    def fetch(i):
        rows = pl.ds(i * part_rows, part_rows)
        return pltpu.make_async_copy(w_ref.at[rows], raw.at[rows], raw_sem.at[i])

    for i in range(parts):
        fetch(i).start()
    held[grid.tile(x, z, y, c)] = enc_ref[...]
    total[...] = jnp.zeros_like(total)
    grid.barrier()

    whole = pl.ds(0, R)
    upper, lower = pl.ds(0, R // 2), pl.ds(R // 2, R // 2)
    at_x = Z
    at_y = at_x + (S - 1) * Z
    at_a = at_y + (Y - 1) * Z
    at_b = at_a + (S - 1) * (Y - 1) * Z
    at_s = at_b + (S - 1) * (Y - 1) * Z

    def move(t, rows, target, slot, part=0):
        return pltpu.make_async_remote_copy(
            src_ref=held.at[(*t, rows)],
            dst_ref=held.at[(*t, rows)],
            send_sem=send_sem.at[slot],
            recv_sem=recv_sem.at[(part, *t)],
            device_id=target,
            device_id_type=MESH,
        )

    def arrived(t, rows=whole, part=0):
        move(t, rows, grid.device(wrap(x + 1, S), z, y, c), 0, part).wait_recv()

    def to_sibling(t, dx, dy, dz):
        return [
            move(t, whole, grid.device(x, z, y, wrap(c + d, C)), at_s + (dx * Y + dy) * Z + dz)
            for d in range(1, C)
        ]

    def spread(dz):
        t = grid.tile(x, wrap(z + dz, Z), y, c)
        copies = [
            move(t, whole, grid.device(wrap(x + d, S), z, y, c), at_x + (d - 1) * Z + dz)
            for d in range(1, S)
        ]
        copies += [
            move(t, whole, grid.device(x, z, wrap(y + d, Y), c), at_y + (d - 1) * Z + dz)
            for d in range(1, Y)
        ]
        return copies + to_sibling(t, 0, 0, dz)

    def pass_x(dx, dz):
        t = grid.tile(wrap(x + dx, S), wrap(z + dz, Z), y, c)
        copies = [
            move(t, upper, grid.device(x, z, wrap(y + d, Y), c),
                 at_a + ((dx - 1) * (Y - 1) + d - 1) * Z + dz, 0)
            for d in range(1, Y)
        ]
        return copies + to_sibling(t, dx, 0, dz)

    def pass_y(dy, dz):
        t = grid.tile(x, wrap(z + dz, Z), wrap(y + dy, Y), c)
        copies = [
            move(t, lower, grid.device(wrap(x + d, S), z, y, c),
                 at_b + ((d - 1) * (Y - 1) + dy - 1) * Z + dz, 1)
            for d in range(1, S)
        ]
        return copies + to_sibling(t, 0, dy, dz)

    def start(copies):
        for copy in copies:
            copy.start()

    def done(copies):
        for copy in copies:
            copy.wait_send()

    own = grid.tile(x, z, y, c)

    def along_z(dz):
        return [move(own, whole, grid.device(x, wrap(z + dz, Z), y, c), dz)]

    each(1, Z, lambda dz: start(along_z(dz)))
    start(spread(0))

    size = 2 * LANES
    count = size // (2 * lane_tiles)
    flat = raw.reshape(depth * lane_tiles * 2, LANES)

    def unpack(low, high):
        def block(i):
            for u in range(UNROLL):
                first = (i * UNROLL + u) * 2
                both = jnp.concatenate(
                    [
                        flat[pl.ds(pl.multiple_of((first + k) * size, size), size), :]
                        for k in range(2)
                    ],
                    axis=1,
                )
                apart = jnp.dot(pick[...], both, preferred_element_type=jnp.float32).astype(
                    jnp.bfloat16
                )
                for k in range(2):
                    row = pl.ds(pl.multiple_of((first + k) * count, count), count)
                    for col in range(2 * lane_tiles):
                        weight[row, col * LANES : (col + 1) * LANES] = apart[
                            col * count : (col + 1) * count, k * LANES : (k + 1) * LANES
                        ]

        each(low, high, block)

    blocks = depth // (count * 2 * UNROLL)
    pick[...] = select(lane_tiles, 0)
    for i in range(parts // 2):
        fetch(i).wait()
    unpack(0, blocks // 2)

    def column(dz):
        arrived(grid.tile(x, wrap(z + dz, Z), y, c))
        start(spread(dz))

    each(1, Z, column)
    for i in range(parts // 2, parts):
        fetch(i).wait()
    unpack(blocks // 2, blocks)
    weight_out = pltpu.make_async_copy(weight, wcat_ref, out_sem.at[0])
    weight_out.start()

    def multiply(tz, ty, tc):
        p = grid.p(tz, ty, tc)
        total[...] += jnp.dot(
            held[:, p].reshape(S * R, F),
            weight[pl.ds(pl.multiple_of(p * F, F), F), :],
            preferred_element_type=jnp.float32,
        )

    def sides(dz):
        tz = wrap(z + dz, Z)
        for dx in range(1, S):
            arrived(grid.tile(wrap(x + dx, S), tz, y, c))
            start(pass_x(dx, dz))
        for dy in range(1, Y):
            arrived(grid.tile(x, tz, wrap(y + dy, Y), c))
            start(pass_y(dy, dz))
        multiply(tz, y, c)

    each(0, Z, sides)

    def diagonal(dz):
        tz = wrap(z + dz, Z)
        for dy in range(1, Y):
            ty = wrap(y + dy, Y)
            for dx in range(1, S):
                t = grid.tile(wrap(x + dx, S), tz, ty, c)
                arrived(t, upper, 0)
                arrived(t, lower, 1)
                start(to_sibling(t, dx, dy, dz))
            multiply(tz, ty, c)

    each(0, Z, diagonal)

    for dc in range(1, C):
        for dy in range(Y):

            def other(dz):
                tz, ty, tc = wrap(z + dz, Z), wrap(y + dy, Y), wrap(c + dc, C)
                for dx in range(S):
                    arrived(grid.tile(wrap(x + dx, S), tz, ty, tc))
                multiply(tz, ty, tc)

            each(0, Z, other)
    states_out = pltpu.make_async_copy(held, states_ref, out_sem.at[1])
    states_out.start()
    kv_ref[...] = total[...].astype(jnp.bfloat16)

    each(1, Z, lambda dz: done(along_z(dz)))

    def sent(dz):
        done(spread(dz))
        for dx in range(1, S):
            done(pass_x(dx, dz))
        for dy in range(1, Y):
            done(pass_y(dy, dz))
        for dx in range(1, S):
            for dy in range(1, Y):
                t = grid.tile(wrap(x + dx, S), wrap(z + dz, Z), wrap(y + dy, Y), c)
                done(to_sibling(t, dx, dy, dz))

    each(0, Z, sent)
    weight_out.wait()
    states_out.wait()


def attention_kernel(len_ref, kv_ref, q_ref, g_ref, ctx_ref, qgrad_ref, kvgrad_ref):
    R = kv_ref.shape[0]
    T, L = q_ref.shape
    heads = L // HD
    limit = len_ref[pl.program_id(0)]
    q, g = q_ref[...], g_ref[...]
    keys, values = kv_ref[:, :L], kv_ref[:, L:]
    column = lax.broadcasted_iota(jnp.int32, (R, L), 1)
    pick = [
        jnp.where((column >= h * HD) & (column < (h + 1) * HD), 1.0, 0.0).astype(jnp.float32)
        for h in range(heads)
    ]
    key_stack = jnp.concatenate([keys * m.astype(jnp.bfloat16) for m in pick], axis=0)
    value_stack = jnp.concatenate([values * m.astype(jnp.bfloat16) for m in pick], axis=0)
    factor = HD ** (-0.5)
    f32 = jnp.float32
    scores = lax.dot_general(key_stack, q, NT, preferred_element_type=f32)
    prob_grad = lax.dot_general(value_stack, g, NT, preferred_element_type=f32)
    valid = lax.broadcasted_iota(jnp.int32, (R, T), 0) < limit
    probs, grads = [], []
    for h in range(heads):
        rows = slice(h * R, (h + 1) * R)
        score = jnp.where(valid, scores[rows] * factor, -1e30)
        exponent = jnp.exp(score - jnp.max(score, axis=0, keepdims=True))
        prob = exponent * (1.0 / jnp.sum(exponent, axis=0, keepdims=True))
        part = prob_grad[rows]
        mean = jnp.sum(part * prob, axis=0, keepdims=True)
        probs.append(prob.astype(jnp.bfloat16))
        grads.append((prob * (part - mean) * factor).astype(jnp.bfloat16))
    prob = jnp.concatenate(probs, axis=0)
    grad = jnp.concatenate(grads, axis=0)

    def own_columns(full):
        return sum(pick[h] * full[h * R : (h + 1) * R] for h in range(heads))

    value_grad = own_columns(jnp.dot(prob, g, preferred_element_type=f32))
    key_grad = own_columns(jnp.dot(grad, q, preferred_element_type=f32))
    kvgrad_ref[:, :L] = key_grad.astype(jnp.bfloat16)
    kvgrad_ref[:, L:] = value_grad.astype(jnp.bfloat16)
    ctx_ref[...] = lax.dot_general(prob, value_stack, TN, preferred_element_type=f32).astype(
        jnp.bfloat16
    )
    qgrad_ref[...] = lax.dot_general(grad, key_stack, TN, preferred_element_type=f32).astype(
        jnp.bfloat16
    )


def scatter_kernel(
    grid, kvgrad_ref, wcat_ref, states_ref, out_ref, wgrad_ref,
    weight, states, packed, pick, mine, away, near, diag_a, diag_b, from_x, from_y, from_z, to_z,
    weight_sem, near_send, near_recv, a_send, a_recv, b_send, b_recv,
    x_send, x_recv, y_send, y_recv, z_send, z_recv, packed_sem,
):
    S, Y, Z, C = grid.S, grid.Y, grid.Z, grid.C
    R, F = out_ref.shape
    x, z, y, c = grid.here()
    bf16, f32 = jnp.bfloat16, jnp.float32
    weight_in = pltpu.make_async_copy(wcat_ref, weight, weight_sem.at[0])
    weight_in.start()
    states_in = pltpu.make_async_copy(states_ref, states, weight_sem.at[1])
    states_in.start()
    pick[...] = select(packed.shape[1] // F, 1)
    grid.barrier()
    weight_in.wait()

    def term(tz, ty, tc):
        row = pl.multiple_of(grid.p(tz, ty, tc) * F, F)
        full = lax.dot_general(
            kvgrad_ref[...], weight[pl.ds(row, F), :], NT, preferred_element_type=f32
        )
        return full.reshape(S, R, F)

    M, tall = packed.shape[:2]
    lane_tiles = tall // F
    size = 2 * LANES
    count = size // (2 * lane_tiles)
    beside = 2 if F % (2 * count) == 0 else 1

    def put(p):
        return pltpu.make_async_copy(
            packed.at[p],
            wgrad_ref.at[pl.ds(pl.multiple_of(p * tall, tall), tall)],
            packed_sem.at[p],
        )

    def weight_block(p):
        full = lax.dot_general(
            states[:, p].reshape(S * R, F), kvgrad_ref[...], TN, preferred_element_type=f32
        ).astype(bf16)
        flat = packed.at[p].reshape(2 * tall, LANES)
        for g in range(0, F // count, beside):
            both = jnp.concatenate(
                [
                    jnp.concatenate(
                        [
                            full[k * count : (k + 1) * count, col * LANES : (col + 1) * LANES]
                            for col in range(2 * lane_tiles)
                        ],
                        axis=0,
                    )
                    for k in range(g, g + beside)
                ],
                axis=1,
            )
            mixed = jnp.dot(pick[...], both, preferred_element_type=f32).astype(bf16)
            for k in range(beside):
                flat[(g + k) * size : (g + k + 1) * size, :] = mixed[
                    :, k * LANES : (k + 1) * LANES
                ]
        put(p).start()

    def remote(src, dst, send, recv, target):
        return pltpu.make_async_remote_copy(
            src_ref=src, dst_ref=dst, send_sem=send, recv_sem=recv,
            device_id=target, device_id_type=MESH,
        )

    def near_copy(i):
        return remote(
            away.at[i], near.at[i], near_send.at[i], near_recv.at[i],
            grid.device(x, z, y, wrap(c + 1, C)),
        )

    def half_a(dx, dy, tz):
        i = ((dy - 1) * (S - 1) + dx - 1) * Z + tz
        ty = wrap(y + dy, Y)
        return remote(
            mine.at[tz * Y + ty, wrap(x + dx, S), pl.ds(0, R // 2)], diag_a.at[i],
            a_send.at[i], a_recv.at[i], grid.device(x, z, ty, c),
        )

    def half_b(dx, dy, tz):
        i = ((dy - 1) * (S - 1) + dx - 1) * Z + tz
        tx = wrap(x + dx, S)
        return remote(
            mine.at[tz * Y + wrap(y + dy, Y), tx, pl.ds(R // 2, R // 2)], diag_b.at[i],
            b_send.at[i], b_recv.at[i], grid.device(tx, z, y, c),
        )

    def along_x(dx, tz):
        i = (dx - 1) * Z + tz
        tx = wrap(x + dx, S)
        return remote(
            mine.at[tz * Y + y, tx], from_x.at[i], x_send.at[i], x_recv.at[i],
            grid.device(tx, z, y, c),
        )

    def along_y(dy, tz):
        i = (dy - 1) * Z + tz
        ty = wrap(y + dy, Y)
        return remote(
            mine.at[tz * Y + ty, x], from_y.at[i], y_send.at[i], y_recv.at[i],
            grid.device(x, z, ty, c),
        )

    def along_z(dz):
        tz = wrap(z + dz, Z)
        return remote(
            to_z.at[dz], from_z.at[dz], z_send.at[dz], z_recv.at[dz],
            grid.device(x, tz, y, c),
        )

    if C > 1:
        for dy in [*range(1, Y), 0]:

            def give(dz):
                tz, ty = wrap(z + dz, Z), wrap(y + dy, Y)
                i = tz * Y + ty
                away[i] = term(tz, ty, wrap(c + 1, C)).astype(bf16)
                near_copy(i).start()

            each(1, Z + 1, give)

    def collect(dz, dy):
        tz, ty = wrap(z + dz, Z), wrap(y + dy, Y)
        i = tz * Y + ty
        value = term(tz, ty, c)
        if C > 1:
            near_copy(i).wait_recv()
            value = value + near[i].astype(f32)
        mine[i] = value.astype(bf16)
        if dy:
            for dx in range(1, S):
                half_a(dx, dy, tz).start()
                half_b(dx, dy, tz).start()

    for dy in [*range(1, Y), 0]:
        each(1, Z + 1, lambda dz: collect(dz, dy))

    states_in.wait()
    first, second = 3 * M // 16, 10 * M // 16
    each(0, first, weight_block)

    def sides(dz):
        tz = wrap(z + dz, Z)
        for dx in range(1, S):
            tx = wrap(x + dx, S)
            for dy in range(1, Y):
                copy = half_a(dx, dy, tz)
                copy.wait_recv()
                i = ((dy - 1) * (S - 1) + dx - 1) * Z + tz
                spot = (tz * Y + y, tx, pl.ds(0, R // 2))
                mine[spot] = (mine[spot].astype(f32) + diag_a[i].astype(f32)).astype(bf16)
            along_x(dx, tz).start()
        for dy in range(1, Y):
            ty = wrap(y + dy, Y)
            for dx in range(1, S):
                half_b(dx, dy, tz).wait_recv()
                i = ((dy - 1) * (S - 1) + dx - 1) * Z + tz
                spot = (tz * Y + ty, x, pl.ds(R // 2, R // 2))
                mine[spot] = (mine[spot].astype(f32) + diag_b[i].astype(f32)).astype(bf16)
            along_y(dy, tz).start()

    each(1, Z + 1, sides)
    each(first, second, weight_block)

    def joined(dz):
        tz = wrap(z + dz, Z)
        value = mine[tz * Y + y, x].astype(f32)
        for dx in range(1, S):
            along_x(dx, tz).wait_recv()
            value = value + from_x[(dx - 1) * Z + tz].astype(f32)
        for dy in range(1, Y):
            along_y(dy, tz).wait_recv()
            value = value + from_y[(dy - 1) * Z + tz].astype(f32)
        return value

    def pass_on(dz):
        to_z[dz] = joined(dz).astype(bf16)
        along_z(dz).start()

    each(1, Z, pass_on)
    each(second, M, weight_block)
    value = joined(0)
    for dz in range(1, Z):
        along_z(dz).wait_recv()
        value = value + from_z[dz].astype(f32)
    out_ref[...] = value.astype(bf16)

    def sent(tz):
        for dy in range(Y):
            if C > 1:
                near_copy(tz * Y + dy).wait_send()
        for dx in range(1, S):
            along_x(dx, tz).wait_send()
            for dy in range(1, Y):
                half_a(dx, dy, tz).wait_send()
                half_b(dx, dy, tz).wait_send()
        for dy in range(1, Y):
            along_y(dy, tz).wait_send()

    each(0, Z, sent)
    each(1, Z, lambda dz: along_z(dz).wait_send())

    def written(p):
        put(p).wait()

    each(0, M, written)


def settle_kernel(from_ref, to_ref, held, in_sem, out_sem):
    parts = in_sem.shape[0]
    part_rows = held.shape[0] // parts

    def copies(i):
        rows = pl.ds(i * part_rows, part_rows)
        return (
            pltpu.make_async_copy(from_ref.at[rows], held.at[rows], in_sem.at[i]),
            pltpu.make_async_copy(held.at[rows], to_ref.at[rows], out_sem.at[i]),
        )

    for i in range(parts):
        copies(i)[0].start()
    for i in range(parts):
        copies(i)[0].wait()
        copies(i)[1].start()
    for i in range(parts):
        copies(i)[1].wait()


def shards(grid, enc_final, enc_len, kv_weight, queries, d_context):
    S, M, C, Y, Z = grid.S, grid.M, grid.C, grid.Y, grid.Z
    R, F = enc_final.shape[1:]
    D, _, L = kv_weight.shape[1:]
    T = queries.shape[2]
    lane_tiles = L // LANES
    bf16, f32 = jnp.bfloat16, jnp.float32
    dma = pltpu.SemaphoreType.DMA
    vmem = pl.BlockSpec(memory_space=pltpu.VMEM)
    anywhere = pl.BlockSpec(memory_space=pl.ANY)
    shape = jax.ShapeDtypeStruct
    by_lane_tile = (
        kv_weight[0].reshape(D, 2, lane_tiles, LANES).transpose(0, 2, 1, 3)
    ).reshape(D * lane_tiles, 2, LANES)
    sends = Z + (S - 1) * Z + (Y - 1) * Z + 2 * (S - 1) * (Y - 1) * Z + S * Y * Z
    states, wcat, key_value = pl.pallas_call(
        functools.partial(gather_kernel, grid),
        out_shape=(
            shape((S, M, R, F), bf16), shape((D, 2 * L), bf16), shape((S * R, 2 * L), bf16),
        ),
        in_specs=[vmem, anywhere],
        out_specs=(anywhere, anywhere, vmem),
        scratch_shapes=[
            pltpu.VMEM((S, M, R, F), bf16),
            pltpu.VMEM((D, 2 * L), bf16),
            pltpu.VMEM((D * lane_tiles, 2, LANES), bf16),
            pltpu.VMEM((2 * LANES, 2 * LANES), bf16),
            pltpu.VMEM((S * R, 2 * L), f32),
            dma((4,)),
            dma((sends,)),
            dma((2, S, M)),
            dma((2,)),
        ],
        compiler_params=pltpu.CompilerParams(
            collective_id=0, has_side_effects=True, vmem_limit_bytes=VMEM_BYTES
        ),
        name="gather_states",
    )(enc_final[0], by_lane_tile)

    rows = pl.BlockSpec((R, 2 * L), lambda m: (m, 0))
    long = pl.BlockSpec((None, T, L), lambda m: (m, 0, 0))
    context, query_grad, kv_grad = pl.pallas_call(
        attention_kernel,
        grid=(S,),
        out_shape=(
            shape((S, T, L), bf16), shape((S, T, L), bf16), shape((S * R, 2 * L), bf16),
        ),
        in_specs=[pl.BlockSpec(memory_space=pltpu.SMEM), rows, long, long],
        out_specs=(long, long, rows),
        compiler_params=pltpu.CompilerParams(vmem_limit_bytes=VMEM_BYTES),
        name="attention",
    )(enc_len, key_value, queries[0], d_context[0])

    pair = max((S - 1) * (Y - 1) * Z, 1)
    enc_grad, weight_grad = pl.pallas_call(
        functools.partial(scatter_kernel, grid),
        out_shape=(shape((R, F), bf16), shape((D * lane_tiles, 2, LANES), bf16)),
        in_specs=[vmem, anywhere, anywhere],
        out_specs=(vmem, anywhere),
        scratch_shapes=[
            pltpu.VMEM((D, 2 * L), bf16),
            pltpu.VMEM((S, M, R, F), bf16),
            pltpu.VMEM((M, F * lane_tiles, 2, LANES), bf16),
            pltpu.VMEM((2 * LANES, 2 * LANES), bf16),
            pltpu.VMEM((Z * Y, S, R, F), bf16),
            pltpu.VMEM((Z * Y, S, R, F), bf16),
            pltpu.VMEM((Z * Y, S, R, F), bf16),
            pltpu.VMEM((pair, R // 2, F), bf16),
            pltpu.VMEM((pair, R // 2, F), bf16),
            pltpu.VMEM((max(S - 1, 1) * Z, R, F), bf16),
            pltpu.VMEM((max(Y - 1, 1) * Z, R, F), bf16),
            pltpu.VMEM((Z, R, F), bf16),
            pltpu.VMEM((Z, R, F), bf16),
            dma((2,)),
            dma((Z * Y,)), dma((Z * Y,)),
            dma((pair,)), dma((pair,)), dma((pair,)), dma((pair,)),
            dma((max(S - 1, 1) * Z,)), dma((max(S - 1, 1) * Z,)),
            dma((max(Y - 1, 1) * Z,)), dma((max(Y - 1, 1) * Z,)),
            dma((Z,)), dma((Z,)), dma((M,)),
        ],
        compiler_params=pltpu.CompilerParams(
            collective_id=1, has_side_effects=True, vmem_limit_bytes=VMEM_BYTES
        ),
        name="scatter_states_grad",
    )(kv_grad, wcat, states)

    weight_grad = pl.pallas_call(
        settle_kernel,
        out_shape=shape((D * lane_tiles, 2, LANES), bf16),
        in_specs=[anywhere],
        out_specs=anywhere,
        scratch_shapes=[pltpu.VMEM((D * lane_tiles, 2, LANES), bf16), dma((8,)), dma((8,))],
        compiler_params=pltpu.CompilerParams(vmem_limit_bytes=VMEM_BYTES),
        name="settle_weight_grad",
    )(weight_grad)
    weight_grad = (
        weight_grad.reshape(D, lane_tiles, 2, LANES).transpose(0, 2, 1, 3).reshape(D, 2, L)
    )
    return context[None], query_grad[None], weight_grad[None], enc_grad[None]


def solution(mesh):
    grid = Grid(mesh.shape["section"], mesh.shape["mp"])
    split = P("section", None, None, "mp")
    return jax.shard_map(
        functools.partial(shards, grid),
        mesh=mesh,
        in_specs=(P("section", None, "mp"), P(), split, split, split),
        out_specs=(split, split, split, P("section", None, "mp")),
        check_vma=False,
    )
```

```python
import functools

import jax
import jax.numpy as jnp
from jax import lax
from jax.experimental import pallas as pl
from jax.experimental.pallas import tpu as pltpu
from jax.sharding import PartitionSpec as P

HD = 64
LANES = 128
MESH = pl.DeviceIdType.MESH
VMEM_BYTES = 56 * 2**20
UNROLL = 4
NT = (((1,), (1,)), ((), ()))
TN = (((0,), (0,)), ((), ()))


def wrap(value, size):
    return lax.rem(value, size)


class Grid:
    def __init__(self, section, mp):
        self.S, self.M = section, mp
        self.C = 2 if mp % 2 == 0 else 1
        self.Y = 2 if (mp // self.C) % 2 == 0 else 1
        self.Z = mp // self.C // self.Y

    def here(self):
        x, p = lax.axis_index("section"), lax.axis_index("mp")
        c = lax.rem(p, self.C)
        zy = lax.div(p, self.C)
        return x, lax.div(zy, self.Y), lax.rem(zy, self.Y), c

    def p(self, z, y, c):
        return (z * self.Y + y) * self.C + c

    def tile(self, x, z, y, c):
        return x, self.p(z, y, c)

    def device(self, x, z, y, c):
        return (x, self.p(z, y, c))

    def barrier(self):
        x, z, y, c = self.here()
        sem = pltpu.get_barrier_semaphore()
        peers = [self.device(wrap(x + d, self.S), z, y, c) for d in range(1, self.S)]
        peers += [self.device(x, wrap(z + d, self.Z), y, c) for d in range(1, self.Z)]
        peers += [self.device(x, z, wrap(y + d, self.Y), c) for d in range(1, self.Y)]
        peers += [self.device(x, z, y, wrap(c + d, self.C)) for d in range(1, self.C)]
        for peer in peers:
            pl.semaphore_signal(sem, inc=1, device_id=peer, device_id_type=MESH)
        pl.semaphore_wait(sem, len(peers))


def each(low, high, body):
    def step(i, carry):
        body(i)
        return carry

    lax.fori_loop(low, high, step, 0)


def select(lane_tiles, back):
    size = 2 * LANES
    count = size // (2 * lane_tiles)
    across = lax.broadcasted_iota(jnp.int32, (size, size), 1 - back)
    along = lax.broadcasted_iota(jnp.int32, (size, size), back)
    hit = jnp.zeros((size, size), jnp.float32)
    for kind in range(2):
        for j in range(lane_tiles):
            low = (kind * lane_tiles + j) * count
            source = (along - low) * (2 * lane_tiles) + 2 * j + kind
            inside = (along >= low) & (along < low + count)
            hit = jnp.where(inside & (across == source), 1.0, hit)
    return hit.astype(jnp.bfloat16)


def gather(
    grid, enc_ref, w_ref, kv_ref, held, weight, raw, pick, total, raw_sem, send_sem, recv_sem,
):
    S, Y, Z, C = grid.S, grid.Y, grid.Z, grid.C
    R, F = enc_ref.shape
    depth = weight.shape[0]
    L = weight.shape[1] // 2
    lane_tiles = L // LANES
    x, z, y, c = grid.here()

    parts = raw_sem.shape[0]
    part_rows = raw.shape[0] // parts

    def fetch(i):
        rows = pl.ds(i * part_rows, part_rows)
        return pltpu.make_async_copy(w_ref.at[rows], raw.at[rows], raw_sem.at[i])

    for i in range(parts):
        fetch(i).start()
    held[grid.tile(x, z, y, c)] = enc_ref[...]
    total[...] = jnp.zeros_like(total)
    grid.barrier()

    whole = pl.ds(0, R)
    upper, lower = pl.ds(0, R // 2), pl.ds(R // 2, R // 2)
    at_x = Z
    at_y = at_x + (S - 1) * Z
    at_a = at_y + (Y - 1) * Z
    at_b = at_a + (S - 1) * (Y - 1) * Z
    at_s = at_b + (S - 1) * (Y - 1) * Z

    def move(t, rows, target, slot, part=0):
        return pltpu.make_async_remote_copy(
            src_ref=held.at[(*t, rows)],
            dst_ref=held.at[(*t, rows)],
            send_sem=send_sem.at[slot],
            recv_sem=recv_sem.at[(part, *t)],
            device_id=target,
            device_id_type=MESH,
        )

    def arrived(t, rows=whole, part=0):
        move(t, rows, grid.device(wrap(x + 1, S), z, y, c), 0, part).wait_recv()

    def to_sibling(t, dx, dy, dz):
        return [
            move(t, whole, grid.device(x, z, y, wrap(c + d, C)), at_s + (dx * Y + dy) * Z + dz)
            for d in range(1, C)
        ]

    def spread(dz):
        t = grid.tile(x, wrap(z + dz, Z), y, c)
        copies = [
            move(t, whole, grid.device(wrap(x + d, S), z, y, c), at_x + (d - 1) * Z + dz)
            for d in range(1, S)
        ]
        copies += [
            move(t, whole, grid.device(x, z, wrap(y + d, Y), c), at_y + (d - 1) * Z + dz)
            for d in range(1, Y)
        ]
        return copies + to_sibling(t, 0, 0, dz)

    def pass_x(dx, dz):
        t = grid.tile(wrap(x + dx, S), wrap(z + dz, Z), y, c)
        copies = [
            move(t, upper, grid.device(x, z, wrap(y + d, Y), c),
                 at_a + ((dx - 1) * (Y - 1) + d - 1) * Z + dz, 0)
            for d in range(1, Y)
        ]
        return copies + to_sibling(t, dx, 0, dz)

    def pass_y(dy, dz):
        t = grid.tile(x, wrap(z + dz, Z), wrap(y + dy, Y), c)
        copies = [
            move(t, lower, grid.device(wrap(x + d, S), z, y, c),
                 at_b + ((d - 1) * (Y - 1) + dy - 1) * Z + dz, 1)
            for d in range(1, S)
        ]
        return copies + to_sibling(t, 0, dy, dz)

    def start(copies):
        for copy in copies:
            copy.start()

    def done(copies):
        for copy in copies:
            copy.wait_send()

    own = grid.tile(x, z, y, c)

    def along_z(dz):
        return [move(own, whole, grid.device(x, wrap(z + dz, Z), y, c), dz)]

    each(1, Z, lambda dz: start(along_z(dz)))
    start(spread(0))

    size = 2 * LANES
    count = size // (2 * lane_tiles)
    flat = raw.reshape(depth * lane_tiles * 2, LANES)

    def unpack(low, high):
        def block(i):
            for u in range(UNROLL):
                first = (i * UNROLL + u) * 2
                both = jnp.concatenate(
                    [
                        flat[pl.ds(pl.multiple_of((first + k) * size, size), size), :]
                        for k in range(2)
                    ],
                    axis=1,
                )
                apart = jnp.dot(pick[...], both, preferred_element_type=jnp.float32).astype(
                    jnp.bfloat16
                )
                for k in range(2):
                    row = pl.ds(pl.multiple_of((first + k) * count, count), count)
                    for col in range(2 * lane_tiles):
                        weight[row, col * LANES : (col + 1) * LANES] = apart[
                            col * count : (col + 1) * count, k * LANES : (k + 1) * LANES
                        ]

        each(low, high, block)

    blocks = depth // (count * 2 * UNROLL)
    pick[...] = select(lane_tiles, 0)
    for i in range(parts // 2):
        fetch(i).wait()
    unpack(0, blocks // 2)

    def column(dz):
        arrived(grid.tile(x, wrap(z + dz, Z), y, c))
        start(spread(dz))

    each(1, Z, column)
    for i in range(parts // 2, parts):
        fetch(i).wait()
    unpack(blocks // 2, blocks)

    def multiply(tz, ty, tc):
        p = grid.p(tz, ty, tc)
        total[...] += jnp.dot(
            held[:, p].reshape(S * R, F),
            weight[pl.ds(pl.multiple_of(p * F, F), F), :],
            preferred_element_type=jnp.float32,
        )

    def sides(dz):
        tz = wrap(z + dz, Z)
        for dx in range(1, S):
            arrived(grid.tile(wrap(x + dx, S), tz, y, c))
            start(pass_x(dx, dz))
        for dy in range(1, Y):
            arrived(grid.tile(x, tz, wrap(y + dy, Y), c))
            start(pass_y(dy, dz))
        multiply(tz, y, c)

    each(0, Z, sides)

    def diagonal(dz):
        tz = wrap(z + dz, Z)
        for dy in range(1, Y):
            ty = wrap(y + dy, Y)
            for dx in range(1, S):
                t = grid.tile(wrap(x + dx, S), tz, ty, c)
                arrived(t, upper, 0)
                arrived(t, lower, 1)
                start(to_sibling(t, dx, dy, dz))
            multiply(tz, ty, c)

    each(0, Z, diagonal)

    for dc in range(1, C):
        for dy in range(Y):

            def other(dz):
                tz, ty, tc = wrap(z + dz, Z), wrap(y + dy, Y), wrap(c + dc, C)
                for dx in range(S):
                    arrived(grid.tile(wrap(x + dx, S), tz, ty, tc))
                multiply(tz, ty, tc)

            each(0, Z, other)
    kv_ref[...] = total[...].astype(jnp.bfloat16)

    def sent(dz):
        done(spread(dz))
        for dx in range(1, S):
            done(pass_x(dx, dz))
        for dy in range(1, Y):
            done(pass_y(dy, dz))
        for dx in range(1, S):
            for dy in range(1, Y):
                t = grid.tile(wrap(x + dx, S), wrap(z + dz, Z), wrap(y + dy, Y), c)
                done(to_sibling(t, dx, dy, dz))

    def finish():
        each(1, Z, lambda dz: done(along_z(dz)))
        each(0, Z, sent)

    return finish


def head_columns(R, L):
    column = lax.broadcasted_iota(jnp.int32, (R, L), 1)
    return [
        jnp.where((column >= h * HD) & (column < (h + 1) * HD), 1.0, 0.0).astype(jnp.float32)
        for h in range(L // HD)
    ]


def stack_heads(block):
    pick = head_columns(*block.shape)
    return jnp.concatenate([block * m.astype(block.dtype) for m in pick], axis=0)


def attention_grads(m, R, len_ref, kv_ref, q_ref, g_ref, prob_ref, grad_ref, kvgrad_ref):
    T, L = q_ref.shape[1:]
    heads = L // HD
    rows = pl.ds(pl.multiple_of(m * R, R), R)
    limit = len_ref[m]
    q, g = q_ref[m], g_ref[m]
    factor = HD ** (-0.5)
    f32 = jnp.float32
    scores = lax.dot_general(stack_heads(kv_ref[rows, :L]), q, NT, preferred_element_type=f32)
    prob_grad = lax.dot_general(
        stack_heads(kv_ref[rows, L:]), g, NT, preferred_element_type=f32
    )
    valid = lax.broadcasted_iota(jnp.int32, (R, T), 0) < limit
    for h in range(heads):
        own = slice(h * R, (h + 1) * R)
        score = jnp.where(valid, scores[own] * factor, -1e30)
        exponent = jnp.exp(score - jnp.max(score, axis=0, keepdims=True))
        prob = exponent * (1.0 / jnp.sum(exponent, axis=0, keepdims=True))
        part = prob_grad[own]
        mean = jnp.sum(part * prob, axis=0, keepdims=True)
        prob_ref[m, own] = prob.astype(jnp.bfloat16)
        grad_ref[m, own] = (prob * (part - mean) * factor).astype(jnp.bfloat16)
    pick = head_columns(R, L)

    def own_columns(full):
        return sum(pick[h] * full[h * R : (h + 1) * R] for h in range(heads))

    value_grad = own_columns(jnp.dot(prob_ref[m], g, preferred_element_type=f32))
    key_grad = own_columns(jnp.dot(grad_ref[m], q, preferred_element_type=f32))
    kvgrad_ref[rows, :L] = key_grad.astype(jnp.bfloat16)
    kvgrad_ref[rows, L:] = value_grad.astype(jnp.bfloat16)


def attention_outputs(m, R, kv_ref, prob_ref, grad_ref, ctx_ref, qgrad_ref):
    L = ctx_ref.shape[2]
    rows = pl.ds(pl.multiple_of(m * R, R), R)
    f32 = jnp.float32
    ctx_ref[m] = lax.dot_general(
        prob_ref[m], stack_heads(kv_ref[rows, L:]), TN, preferred_element_type=f32
    ).astype(jnp.bfloat16)
    qgrad_ref[m] = lax.dot_general(
        grad_ref[m], stack_heads(kv_ref[rows, :L]), TN, preferred_element_type=f32
    ).astype(jnp.bfloat16)


def scatter(
    grid, kvgrad_ref, out_ref, wgrad_ref, while_moving,
    weight, states, packed, pick, mine, away, near, diag_a, diag_b, from_x, from_y, from_z, to_z,
    near_send, near_recv, a_send, a_recv, b_send, b_recv,
    x_send, x_recv, y_send, y_recv, z_send, z_recv, packed_sem,
):
    S, Y, Z, C = grid.S, grid.Y, grid.Z, grid.C
    R, F = out_ref.shape
    x, z, y, c = grid.here()
    bf16, f32 = jnp.bfloat16, jnp.float32
    pick[...] = select(packed.shape[1] // F, 1)

    def term(tz, ty, tc):
        row = pl.multiple_of(grid.p(tz, ty, tc) * F, F)
        full = lax.dot_general(
            kvgrad_ref[...], weight[pl.ds(row, F), :], NT, preferred_element_type=f32
        )
        return full.reshape(S, R, F)

    M, tall = packed.shape[:2]
    lane_tiles = tall // F
    size = 2 * LANES
    count = size // (2 * lane_tiles)
    beside = 2 if F % (2 * count) == 0 else 1

    def put(p):
        return pltpu.make_async_copy(
            packed.at[p],
            wgrad_ref.at[pl.ds(pl.multiple_of(p * tall, tall), tall)],
            packed_sem.at[p],
        )

    def weight_block(p):
        full = lax.dot_general(
            states[:, p].reshape(S * R, F), kvgrad_ref[...], TN, preferred_element_type=f32
        ).astype(bf16)
        flat = packed.at[p].reshape(2 * tall, LANES)
        for g in range(0, F // count, beside):
            both = jnp.concatenate(
                [
                    jnp.concatenate(
                        [
                            full[k * count : (k + 1) * count, col * LANES : (col + 1) * LANES]
                            for col in range(2 * lane_tiles)
                        ],
                        axis=0,
                    )
                    for k in range(g, g + beside)
                ],
                axis=1,
            )
            mixed = jnp.dot(pick[...], both, preferred_element_type=f32).astype(bf16)
            for k in range(beside):
                flat[(g + k) * size : (g + k + 1) * size, :] = mixed[
                    :, k * LANES : (k + 1) * LANES
                ]
        put(p).start()

    def remote(src, dst, send, recv, target):
        return pltpu.make_async_remote_copy(
            src_ref=src, dst_ref=dst, send_sem=send, recv_sem=recv,
            device_id=target, device_id_type=MESH,
        )

    def near_copy(i):
        return remote(
            away.at[i], near.at[i], near_send.at[i], near_recv.at[i],
            grid.device(x, z, y, wrap(c + 1, C)),
        )

    def half_a(dx, dy, tz):
        i = ((dy - 1) * (S - 1) + dx - 1) * Z + tz
        ty = wrap(y + dy, Y)
        return remote(
            mine.at[tz * Y + ty, wrap(x + dx, S), pl.ds(0, R // 2)], diag_a.at[i],
            a_send.at[i], a_recv.at[i], grid.device(x, z, ty, c),
        )

    def half_b(dx, dy, tz):
        i = ((dy - 1) * (S - 1) + dx - 1) * Z + tz
        tx = wrap(x + dx, S)
        return remote(
            mine.at[tz * Y + wrap(y + dy, Y), tx, pl.ds(R // 2, R // 2)], diag_b.at[i],
            b_send.at[i], b_recv.at[i], grid.device(tx, z, y, c),
        )

    def along_x(dx, tz):
        i = (dx - 1) * Z + tz
        tx = wrap(x + dx, S)
        return remote(
            mine.at[tz * Y + y, tx], from_x.at[i], x_send.at[i], x_recv.at[i],
            grid.device(tx, z, y, c),
        )

    def along_y(dy, tz):
        i = (dy - 1) * Z + tz
        ty = wrap(y + dy, Y)
        return remote(
            mine.at[tz * Y + ty, x], from_y.at[i], y_send.at[i], y_recv.at[i],
            grid.device(x, z, ty, c),
        )

    def along_z(dz):
        tz = wrap(z + dz, Z)
        return remote(
            to_z.at[dz], from_z.at[dz], z_send.at[dz], z_recv.at[dz],
            grid.device(x, tz, y, c),
        )

    if C > 1:
        for dy in [*range(1, Y), 0]:

            def give(dz):
                tz, ty = wrap(z + dz, Z), wrap(y + dy, Y)
                i = tz * Y + ty
                away[i] = term(tz, ty, wrap(c + 1, C)).astype(bf16)
                near_copy(i).start()

            each(1, Z + 1, give)

    def collect(dz, dy):
        tz, ty = wrap(z + dz, Z), wrap(y + dy, Y)
        i = tz * Y + ty
        value = term(tz, ty, c)
        if C > 1:
            near_copy(i).wait_recv()
            value = value + near[i].astype(f32)
        mine[i] = value.astype(bf16)
        if dy:
            for dx in range(1, S):
                half_a(dx, dy, tz).start()
                half_b(dx, dy, tz).start()

    for dy in [*range(1, Y), 0]:
        each(1, Z + 1, lambda dz: collect(dz, dy))

    while_moving()
    first, second = 3 * M // 16, 10 * M // 16
    each(0, first, weight_block)

    def sides(dz):
        tz = wrap(z + dz, Z)
        for dx in range(1, S):
            tx = wrap(x + dx, S)
            for dy in range(1, Y):
                copy = half_a(dx, dy, tz)
                copy.wait_recv()
                i = ((dy - 1) * (S - 1) + dx - 1) * Z + tz
                spot = (tz * Y + y, tx, pl.ds(0, R // 2))
                mine[spot] = (mine[spot].astype(f32) + diag_a[i].astype(f32)).astype(bf16)
            along_x(dx, tz).start()
        for dy in range(1, Y):
            ty = wrap(y + dy, Y)
            for dx in range(1, S):
                half_b(dx, dy, tz).wait_recv()
                i = ((dy - 1) * (S - 1) + dx - 1) * Z + tz
                spot = (tz * Y + ty, x, pl.ds(R // 2, R // 2))
                mine[spot] = (mine[spot].astype(f32) + diag_b[i].astype(f32)).astype(bf16)
            along_y(dy, tz).start()

    each(1, Z + 1, sides)
    each(first, second, weight_block)

    def joined(dz):
        tz = wrap(z + dz, Z)
        value = mine[tz * Y + y, x].astype(f32)
        for dx in range(1, S):
            along_x(dx, tz).wait_recv()
            value = value + from_x[(dx - 1) * Z + tz].astype(f32)
        for dy in range(1, Y):
            along_y(dy, tz).wait_recv()
            value = value + from_y[(dy - 1) * Z + tz].astype(f32)
        return value

    def pass_on(dz):
        to_z[dz] = joined(dz).astype(bf16)
        along_z(dz).start()

    each(1, Z, pass_on)
    each(second, M, weight_block)
    value = joined(0)
    for dz in range(1, Z):
        along_z(dz).wait_recv()
        value = value + from_z[dz].astype(f32)
    out_ref[...] = value.astype(bf16)

    def sent(tz):
        for dy in range(Y):
            if C > 1:
                near_copy(tz * Y + dy).wait_send()
        for dx in range(1, S):
            along_x(dx, tz).wait_send()
            for dy in range(1, Y):
                half_a(dx, dy, tz).wait_send()
                half_b(dx, dy, tz).wait_send()
        for dy in range(1, Y):
            along_y(dy, tz).wait_send()

    each(0, Z, sent)
    each(1, Z, lambda dz: along_z(dz).wait_send())

    def written(p):
        put(p).wait()

    each(0, M, written)


def fused_kernel(
    grid, len_ref, enc_ref, w_ref, q_in, g_in,
    ctx_out, qgrad_out, enc_out, wgrad_out,
    kv, q, g, ctx, qgrad, prob, grad, kvgrad, local_sem,
    held, weight, raw, pick, total, raw_sem, send_sem, recv_sem,
    packed, mix, *rest,
):
    R = enc_ref.shape[0]

    def local(src, dst, i):
        return pltpu.make_async_copy(src, dst, local_sem.at[i])

    local(q_in, q, 0).start()
    local(g_in, g, 1).start()
    finish = gather(
        grid, enc_ref, w_ref, kv, held, weight, raw, pick, total, raw_sem, send_sem, recv_sem
    )
    local(q_in, q, 0).wait()
    local(g_in, g, 1).wait()
    each(
        0, grid.S,
        lambda m: attention_grads(m, R, len_ref, kv, q, g, prob, grad, kvgrad),
    )

    def while_moving():
        each(0, grid.S, lambda m: attention_outputs(m, R, kv, prob, grad, ctx, qgrad))
        local(ctx, ctx_out, 2).start()
        local(qgrad, qgrad_out, 3).start()

    scatter(grid, kvgrad, enc_out, wgrad_out, while_moving, weight, held, packed, mix, *rest)
    local(ctx, ctx_out, 2).wait()
    local(qgrad, qgrad_out, 3).wait()
    finish()


def settle_kernel(count, *refs):
    sources, targets, buffers = refs[:count], refs[count : 2 * count], refs[2 * count : -2]
    in_sem, out_sem = refs[-2:]
    plan = []
    for source, target, buffer in zip(sources, targets, buffers):
        parts = 8 if source.shape[0] % 8 == 0 else 1
        step = source.shape[0] // parts
        plan += [(source, target, buffer, pl.ds(i * step, step)) for i in range(parts)]

    def load(i):
        source, _, buffer, rows = plan[i]
        return pltpu.make_async_copy(source.at[rows], buffer.at[rows], in_sem.at[i])

    def store(i):
        _, target, buffer, rows = plan[i]
        return pltpu.make_async_copy(buffer.at[rows], target.at[rows], out_sem.at[i])

    for i in range(len(plan)):
        load(i).start()
    for i in range(len(plan)):
        load(i).wait()
        store(i).start()
    for i in range(len(plan)):
        store(i).wait()


def shards(grid, enc_final, enc_len, kv_weight, queries, d_context):
    S, M, C, Y, Z = grid.S, grid.M, grid.C, grid.Y, grid.Z
    R, F = enc_final.shape[1:]
    D, _, L = kv_weight.shape[1:]
    T = queries.shape[2]
    lane_tiles = L // LANES
    bf16, f32 = jnp.bfloat16, jnp.float32
    dma = pltpu.SemaphoreType.DMA
    vmem = pl.BlockSpec(memory_space=pltpu.VMEM)
    anywhere = pl.BlockSpec(memory_space=pl.ANY)
    shape = jax.ShapeDtypeStruct
    by_lane_tile = (
        kv_weight[0].reshape(D, 2, lane_tiles, LANES).transpose(0, 2, 1, 3)
    ).reshape(D * lane_tiles, 2, LANES)
    sends = Z + (S - 1) * Z + (Y - 1) * Z + 2 * (S - 1) * (Y - 1) * Z + S * Y * Z
    pair = max((S - 1) * (Y - 1) * Z, 1)
    heads = L // HD
    results = (
        shape((S, T, L), bf16), shape((S, T, L), bf16),
        shape((R, F), bf16), shape((D * lane_tiles, 2, LANES), bf16),
    )
    partial = pl.pallas_call(
        functools.partial(fused_kernel, grid),
        out_shape=results,
        in_specs=[pl.BlockSpec(memory_space=pltpu.SMEM), vmem, anywhere, anywhere, anywhere],
        out_specs=(anywhere, anywhere, vmem, anywhere),
        scratch_shapes=[
            pltpu.VMEM((S * R, 2 * L), bf16),
            pltpu.VMEM((S, T, L), bf16),
            pltpu.VMEM((S, T, L), bf16),
            pltpu.VMEM((S, T, L), bf16),
            pltpu.VMEM((S, T, L), bf16),
            pltpu.VMEM((S, heads * R, T), bf16),
            pltpu.VMEM((S, heads * R, T), bf16),
            pltpu.VMEM((S * R, 2 * L), bf16),
            dma((4,)),
            pltpu.VMEM((S, M, R, F), bf16),
            pltpu.VMEM((D, 2 * L), bf16),
            pltpu.VMEM((D * lane_tiles, 2, LANES), bf16),
            pltpu.VMEM((2 * LANES, 2 * LANES), bf16),
            pltpu.VMEM((S * R, 2 * L), f32),
            dma((4,)),
            dma((sends,)),
            dma((2, S, M)),
            pltpu.VMEM((M, F * lane_tiles, 2, LANES), bf16),
            pltpu.VMEM((2 * LANES, 2 * LANES), bf16),
            pltpu.VMEM((Z * Y, S, R, F), bf16),
            pltpu.VMEM((Z * Y, S, R, F), bf16),
            pltpu.VMEM((Z * Y, S, R, F), bf16),
            pltpu.VMEM((pair, R // 2, F), bf16),
            pltpu.VMEM((pair, R // 2, F), bf16),
            pltpu.VMEM((max(S - 1, 1) * Z, R, F), bf16),
            pltpu.VMEM((max(Y - 1, 1) * Z, R, F), bf16),
            pltpu.VMEM((Z, R, F), bf16),
            pltpu.VMEM((Z, R, F), bf16),
            dma((Z * Y,)), dma((Z * Y,)),
            dma((pair,)), dma((pair,)), dma((pair,)), dma((pair,)),
            dma((max(S - 1, 1) * Z,)), dma((max(S - 1, 1) * Z,)),
            dma((max(Y - 1, 1) * Z,)), dma((max(Y - 1, 1) * Z,)),
            dma((Z,)), dma((Z,)), dma((M,)),
        ],
        compiler_params=pltpu.CompilerParams(
            collective_id=0, has_side_effects=True, vmem_limit_bytes=VMEM_BYTES
        ),
        name="cross_attention",
    )(enc_len, enc_final[0], by_lane_tile, queries[0], d_context[0])

    context, query_grad, enc_grad, weight_grad = pl.pallas_call(
        functools.partial(settle_kernel, len(results)),
        out_shape=results,
        in_specs=[anywhere] * len(results),
        out_specs=(anywhere,) * len(results),
        scratch_shapes=[
            *(pltpu.VMEM(r.shape, r.dtype) for r in results),
            dma((8 * len(results),)),
            dma((8 * len(results),)),
        ],
        compiler_params=pltpu.CompilerParams(vmem_limit_bytes=VMEM_BYTES),
        name="settle_results",
    )(*partial)
    weight_grad = (
        weight_grad.reshape(D, lane_tiles, 2, LANES).transpose(0, 2, 1, 3).reshape(D, 2, L)
    )
    return context[None], query_grad[None], weight_grad[None], enc_grad[None]


def solution(mesh):
    grid = Grid(mesh.shape["section"], mesh.shape["mp"])
    split = P("section", None, None, "mp")
    return jax.shard_map(
        functools.partial(shards, grid),
        mesh=mesh,
        in_specs=(P("section", None, "mp"), P(), split, split, split),
        out_specs=(split, split, split, P("section", None, "mp")),
        check_vma=False,
    )
```

```python
import functools

import jax
import jax.numpy as jnp
from jax import lax
from jax.experimental import pallas as pl
from jax.experimental.pallas import tpu as pltpu
from jax.sharding import PartitionSpec as P

HD = 64
LANES = 128
MESH = pl.DeviceIdType.MESH
VMEM_BYTES = 56 * 2**20
UNROLL = 4
NT = (((1,), (1,)), ((), ()))
TN = (((0,), (0,)), ((), ()))


def wrap(value, size):
    return lax.rem(value, size)


class Grid:
    def __init__(self, section, mp):
        self.S, self.M = section, mp
        self.C = 2 if mp % 2 == 0 else 1
        self.Y = 2 if (mp // self.C) % 2 == 0 else 1
        self.Z = mp // self.C // self.Y

    def here(self):
        x, p = lax.axis_index("section"), lax.axis_index("mp")
        c = lax.rem(p, self.C)
        zy = lax.div(p, self.C)
        return x, lax.div(zy, self.Y), lax.rem(zy, self.Y), c

    def p(self, z, y, c):
        return (z * self.Y + y) * self.C + c

    def tile(self, x, z, y, c):
        return x, self.p(z, y, c)

    def device(self, x, z, y, c):
        return (x, self.p(z, y, c))

    def barrier(self):
        x, z, y, c = self.here()
        sem = pltpu.get_barrier_semaphore()
        peers = [self.device(wrap(x + d, self.S), z, y, c) for d in range(1, self.S)]
        peers += [self.device(x, wrap(z + d, self.Z), y, c) for d in range(1, self.Z)]
        peers += [self.device(x, z, wrap(y + d, self.Y), c) for d in range(1, self.Y)]
        peers += [self.device(x, z, y, wrap(c + d, self.C)) for d in range(1, self.C)]
        for peer in peers:
            pl.semaphore_signal(sem, inc=1, device_id=peer, device_id_type=MESH)
        pl.semaphore_wait(sem, len(peers))


def each(low, high, body):
    def step(i, carry):
        body(i)
        return carry

    lax.fori_loop(low, high, step, 0)


def select(lane_tiles, back):
    size = 2 * LANES
    count = size // (2 * lane_tiles)
    across = lax.broadcasted_iota(jnp.int32, (size, size), 1 - back)
    along = lax.broadcasted_iota(jnp.int32, (size, size), back)
    hit = jnp.zeros((size, size), jnp.float32)
    for kind in range(2):
        for j in range(lane_tiles):
            low = (kind * lane_tiles + j) * count
            source = (along - low) * (2 * lane_tiles) + 2 * j + kind
            inside = (along >= low) & (along < low + count)
            hit = jnp.where(inside & (across == source), 1.0, hit)
    return hit.astype(jnp.bfloat16)


def gather(
    grid, enc_ref, w_ref, kv_ref, held, weight, raw, pick, total, raw_sem, send_sem, recv_sem,
):
    S, Y, Z, C = grid.S, grid.Y, grid.Z, grid.C
    R, F = enc_ref.shape
    depth = weight.shape[0]
    L = weight.shape[1] // 2
    lane_tiles = L // LANES
    x, z, y, c = grid.here()

    parts = raw_sem.shape[0]
    part_rows = raw.shape[0] // parts

    def fetch(i):
        rows = pl.ds(i * part_rows, part_rows)
        return pltpu.make_async_copy(w_ref.at[rows], raw.at[rows], raw_sem.at[i])

    for i in range(parts):
        fetch(i).start()
    held[grid.tile(x, z, y, c)] = enc_ref[...]
    total[...] = jnp.zeros_like(total)
    grid.barrier()

    whole = pl.ds(0, R)
    upper, lower = pl.ds(0, R // 2), pl.ds(R // 2, R // 2)
    at_x = Z
    at_y = at_x + (S - 1) * Z
    at_a = at_y + (Y - 1) * Z
    at_b = at_a + (S - 1) * (Y - 1) * Z
    at_s = at_b + (S - 1) * (Y - 1) * Z

    def move(t, rows, target, slot, part=0):
        return pltpu.make_async_remote_copy(
            src_ref=held.at[(*t, rows)],
            dst_ref=held.at[(*t, rows)],
            send_sem=send_sem.at[slot],
            recv_sem=recv_sem.at[(part, *t)],
            device_id=target,
            device_id_type=MESH,
        )

    def arrived(t, rows=whole, part=0):
        move(t, rows, grid.device(wrap(x + 1, S), z, y, c), 0, part).wait_recv()

    def to_sibling(t, dx, dy, dz):
        return [
            move(t, whole, grid.device(x, z, y, wrap(c + d, C)), at_s + (dx * Y + dy) * Z + dz)
            for d in range(1, C)
        ]

    def spread(dz):
        t = grid.tile(x, wrap(z + dz, Z), y, c)
        copies = [
            move(t, whole, grid.device(wrap(x + d, S), z, y, c), at_x + (d - 1) * Z + dz)
            for d in range(1, S)
        ]
        copies += [
            move(t, whole, grid.device(x, z, wrap(y + d, Y), c), at_y + (d - 1) * Z + dz)
            for d in range(1, Y)
        ]
        return copies + to_sibling(t, 0, 0, dz)

    def pass_x(dx, dz):
        t = grid.tile(wrap(x + dx, S), wrap(z + dz, Z), y, c)
        copies = [
            move(t, upper, grid.device(x, z, wrap(y + d, Y), c),
                 at_a + ((dx - 1) * (Y - 1) + d - 1) * Z + dz, 0)
            for d in range(1, Y)
        ]
        return copies + to_sibling(t, dx, 0, dz)

    def pass_y(dy, dz):
        t = grid.tile(x, wrap(z + dz, Z), wrap(y + dy, Y), c)
        copies = [
            move(t, lower, grid.device(wrap(x + d, S), z, y, c),
                 at_b + ((d - 1) * (Y - 1) + dy - 1) * Z + dz, 1)
            for d in range(1, S)
        ]
        return copies + to_sibling(t, 0, dy, dz)

    def start(copies):
        for copy in copies:
            copy.start()

    def done(copies):
        for copy in copies:
            copy.wait_send()

    own = grid.tile(x, z, y, c)

    def along_z(dz):
        return [move(own, whole, grid.device(x, wrap(z + dz, Z), y, c), dz)]

    each(1, Z, lambda dz: start(along_z(dz)))
    start(spread(0))

    size = 2 * LANES
    count = size // (2 * lane_tiles)
    flat = raw.reshape(depth * lane_tiles * 2, LANES)

    def unpack(low, high):
        def block(i):
            for u in range(UNROLL):
                first = (i * UNROLL + u) * 2
                both = jnp.concatenate(
                    [
                        flat[pl.ds(pl.multiple_of((first + k) * size, size), size), :]
                        for k in range(2)
                    ],
                    axis=1,
                )
                apart = jnp.dot(pick[...], both, preferred_element_type=jnp.float32).astype(
                    jnp.bfloat16
                )
                for k in range(2):
                    row = pl.ds(pl.multiple_of((first + k) * count, count), count)
                    for col in range(2 * lane_tiles):
                        weight[row, col * LANES : (col + 1) * LANES] = apart[
                            col * count : (col + 1) * count, k * LANES : (k + 1) * LANES
                        ]

        each(low, high, block)

    blocks = depth // (count * 2 * UNROLL)
    pick[...] = select(lane_tiles, 0)
    for i in range(parts // 2):
        fetch(i).wait()
    unpack(0, blocks // 2)

    def column(dz):
        arrived(grid.tile(x, wrap(z + dz, Z), y, c))
        start(spread(dz))

    each(1, Z, column)

    def multiply(tz, ty, tc):
        p = grid.p(tz, ty, tc)
        total[...] += jnp.dot(
            held[:, p].reshape(S * R, F),
            weight[pl.ds(pl.multiple_of(p * F, F), F), :],
            preferred_element_type=jnp.float32,
        )

    def sides(dz):
        tz = wrap(z + dz, Z)
        for dx in range(1, S):
            arrived(grid.tile(wrap(x + dx, S), tz, y, c))
            start(pass_x(dx, dz))
        for dy in range(1, Y):
            arrived(grid.tile(x, tz, wrap(y + dy, Y), c))
            start(pass_y(dy, dz))

    each(0, Z, sides)
    for i in range(parts // 2, parts):
        fetch(i).wait()
    unpack(blocks // 2, blocks)
    each(0, Z, lambda dz: multiply(wrap(z + dz, Z), y, c))

    def diagonal(dz):
        tz = wrap(z + dz, Z)
        for dy in range(1, Y):
            ty = wrap(y + dy, Y)
            for dx in range(1, S):
                t = grid.tile(wrap(x + dx, S), tz, ty, c)
                arrived(t, upper, 0)
                arrived(t, lower, 1)
                start(to_sibling(t, dx, dy, dz))
            multiply(tz, ty, c)

    each(0, Z, diagonal)

    for dc in range(1, C):
        for dy in range(Y):

            def other(dz):
                tz, ty, tc = wrap(z + dz, Z), wrap(y + dy, Y), wrap(c + dc, C)
                for dx in range(S):
                    arrived(grid.tile(wrap(x + dx, S), tz, ty, tc))
                multiply(tz, ty, tc)

            each(0, Z, other)
    kv_ref[...] = total[...].astype(jnp.bfloat16)

    def sent(dz):
        done(spread(dz))
        for dx in range(1, S):
            done(pass_x(dx, dz))
        for dy in range(1, Y):
            done(pass_y(dy, dz))
        for dx in range(1, S):
            for dy in range(1, Y):
                t = grid.tile(wrap(x + dx, S), wrap(z + dz, Z), wrap(y + dy, Y), c)
                done(to_sibling(t, dx, dy, dz))

    def finish():
        each(1, Z, lambda dz: done(along_z(dz)))
        each(0, Z, sent)

    return finish


def head_columns(R, L):
    column = lax.broadcasted_iota(jnp.int32, (R, L), 1)
    return [
        jnp.where((column >= h * HD) & (column < (h + 1) * HD), 1.0, 0.0).astype(jnp.float32)
        for h in range(L // HD)
    ]


def stack_heads(block):
    pick = head_columns(*block.shape)
    return jnp.concatenate([block * m.astype(block.dtype) for m in pick], axis=0)


def attention_grads(m, R, len_ref, kv_ref, q_ref, g_ref, prob_ref, grad_ref, kvgrad_ref):
    T, L = q_ref.shape[1:]
    heads = L // HD
    rows = pl.ds(pl.multiple_of(m * R, R), R)
    limit = len_ref[m]
    q, g = q_ref[m], g_ref[m]
    factor = HD ** (-0.5)
    f32 = jnp.float32
    scores = lax.dot_general(stack_heads(kv_ref[rows, :L]), q, NT, preferred_element_type=f32)
    prob_grad = lax.dot_general(
        stack_heads(kv_ref[rows, L:]), g, NT, preferred_element_type=f32
    )
    valid = lax.broadcasted_iota(jnp.int32, (R, T), 0) < limit
    for h in range(heads):
        own = slice(h * R, (h + 1) * R)
        score = jnp.where(valid, scores[own] * factor, -1e30)
        exponent = jnp.exp(score - jnp.max(score, axis=0, keepdims=True))
        prob = exponent * (1.0 / jnp.sum(exponent, axis=0, keepdims=True))
        part = prob_grad[own]
        mean = jnp.sum(part * prob, axis=0, keepdims=True)
        prob_ref[m, own] = prob.astype(jnp.bfloat16)
        grad_ref[m, own] = (prob * (part - mean) * factor).astype(jnp.bfloat16)
    pick = head_columns(R, L)

    def own_columns(full):
        return sum(pick[h] * full[h * R : (h + 1) * R] for h in range(heads))

    value_grad = own_columns(jnp.dot(prob_ref[m], g, preferred_element_type=f32))
    key_grad = own_columns(jnp.dot(grad_ref[m], q, preferred_element_type=f32))
    kvgrad_ref[rows, :L] = key_grad.astype(jnp.bfloat16)
    kvgrad_ref[rows, L:] = value_grad.astype(jnp.bfloat16)


def attention_outputs(m, R, kv_ref, prob_ref, grad_ref, ctx_ref, qgrad_ref):
    L = ctx_ref.shape[2]
    rows = pl.ds(pl.multiple_of(m * R, R), R)
    f32 = jnp.float32
    ctx_ref[m] = lax.dot_general(
        prob_ref[m], stack_heads(kv_ref[rows, L:]), TN, preferred_element_type=f32
    ).astype(jnp.bfloat16)
    qgrad_ref[m] = lax.dot_general(
        grad_ref[m], stack_heads(kv_ref[rows, :L]), TN, preferred_element_type=f32
    ).astype(jnp.bfloat16)


def scatter(
    grid, kvgrad_ref, out_ref, wgrad_ref, while_moving,
    weight, states, packed, pick, mine, away, near, diag_a, diag_b, from_x, from_y, from_z, to_z,
    near_send, near_recv, a_send, a_recv, b_send, b_recv,
    x_send, x_recv, y_send, y_recv, z_send, z_recv, packed_sem,
):
    S, Y, Z, C = grid.S, grid.Y, grid.Z, grid.C
    R, F = out_ref.shape
    x, z, y, c = grid.here()
    bf16, f32 = jnp.bfloat16, jnp.float32
    pick[...] = select(packed.shape[1] // F, 1)

    def term(tz, ty, tc):
        row = pl.multiple_of(grid.p(tz, ty, tc) * F, F)
        full = lax.dot_general(
            kvgrad_ref[...], weight[pl.ds(row, F), :], NT, preferred_element_type=f32
        )
        return full.reshape(S, R, F)

    M, tall = packed.shape[:2]
    lane_tiles = tall // F
    size = 2 * LANES
    count = size // (2 * lane_tiles)
    beside = 2 if F % (2 * count) == 0 else 1

    def put(p):
        return pltpu.make_async_copy(
            packed.at[p],
            wgrad_ref.at[pl.ds(pl.multiple_of(p * tall, tall), tall)],
            packed_sem.at[p],
        )

    def weight_block(p):
        full = lax.dot_general(
            states[:, p].reshape(S * R, F), kvgrad_ref[...], TN, preferred_element_type=f32
        ).astype(bf16)
        flat = packed.at[p].reshape(2 * tall, LANES)
        for g in range(0, F // count, beside):
            both = jnp.concatenate(
                [
                    jnp.concatenate(
                        [
                            full[k * count : (k + 1) * count, col * LANES : (col + 1) * LANES]
                            for col in range(2 * lane_tiles)
                        ],
                        axis=0,
                    )
                    for k in range(g, g + beside)
                ],
                axis=1,
            )
            mixed = jnp.dot(pick[...], both, preferred_element_type=f32).astype(bf16)
            for k in range(beside):
                flat[(g + k) * size : (g + k + 1) * size, :] = mixed[
                    :, k * LANES : (k + 1) * LANES
                ]
        put(p).start()

    def remote(src, dst, send, recv, target):
        return pltpu.make_async_remote_copy(
            src_ref=src, dst_ref=dst, send_sem=send, recv_sem=recv,
            device_id=target, device_id_type=MESH,
        )

    def near_copy(i):
        return remote(
            away.at[i], near.at[i], near_send.at[i], near_recv.at[i],
            grid.device(x, z, y, wrap(c + 1, C)),
        )

    def half_a(dx, dy, tz):
        i = ((dy - 1) * (S - 1) + dx - 1) * Z + tz
        ty = wrap(y + dy, Y)
        return remote(
            mine.at[tz * Y + ty, wrap(x + dx, S), pl.ds(0, R // 2)], diag_a.at[i],
            a_send.at[i], a_recv.at[i], grid.device(x, z, ty, c),
        )

    def half_b(dx, dy, tz):
        i = ((dy - 1) * (S - 1) + dx - 1) * Z + tz
        tx = wrap(x + dx, S)
        return remote(
            mine.at[tz * Y + wrap(y + dy, Y), tx, pl.ds(R // 2, R // 2)], diag_b.at[i],
            b_send.at[i], b_recv.at[i], grid.device(tx, z, y, c),
        )

    def along_x(dx, tz):
        i = (dx - 1) * Z + tz
        tx = wrap(x + dx, S)
        return remote(
            mine.at[tz * Y + y, tx], from_x.at[i], x_send.at[i], x_recv.at[i],
            grid.device(tx, z, y, c),
        )

    def along_y(dy, tz):
        i = (dy - 1) * Z + tz
        ty = wrap(y + dy, Y)
        return remote(
            mine.at[tz * Y + ty, x], from_y.at[i], y_send.at[i], y_recv.at[i],
            grid.device(x, z, ty, c),
        )

    def along_z(dz):
        tz = wrap(z + dz, Z)
        return remote(
            to_z.at[dz], from_z.at[dz], z_send.at[dz], z_recv.at[dz],
            grid.device(x, tz, y, c),
        )

    if C > 1:
        for dy in [*range(1, Y), 0]:

            def give(dz):
                tz, ty = wrap(z + dz, Z), wrap(y + dy, Y)
                i = tz * Y + ty
                away[i] = term(tz, ty, wrap(c + 1, C)).astype(bf16)
                near_copy(i).start()

            each(1, Z + 1, give)

    def collect(dz, dy):
        tz, ty = wrap(z + dz, Z), wrap(y + dy, Y)
        i = tz * Y + ty
        value = term(tz, ty, c)
        if C > 1:
            near_copy(i).wait_recv()
            value = value + near[i].astype(f32)
        mine[i] = value.astype(bf16)
        if dy:
            for dx in range(1, S):
                half_a(dx, dy, tz).start()
                half_b(dx, dy, tz).start()

    for dy in [*range(1, Y), 0]:
        each(1, Z + 1, lambda dz: collect(dz, dy))

    while_moving()
    first, second = 3 * M // 16, 10 * M // 16
    each(0, first, weight_block)

    def sides(dz):
        tz = wrap(z + dz, Z)
        for dx in range(1, S):
            tx = wrap(x + dx, S)
            for dy in range(1, Y):
                copy = half_a(dx, dy, tz)
                copy.wait_recv()
                i = ((dy - 1) * (S - 1) + dx - 1) * Z + tz
                spot = (tz * Y + y, tx, pl.ds(0, R // 2))
                mine[spot] = (mine[spot].astype(f32) + diag_a[i].astype(f32)).astype(bf16)
            along_x(dx, tz).start()
        for dy in range(1, Y):
            ty = wrap(y + dy, Y)
            for dx in range(1, S):
                half_b(dx, dy, tz).wait_recv()
                i = ((dy - 1) * (S - 1) + dx - 1) * Z + tz
                spot = (tz * Y + ty, x, pl.ds(R // 2, R // 2))
                mine[spot] = (mine[spot].astype(f32) + diag_b[i].astype(f32)).astype(bf16)
            along_y(dy, tz).start()

    each(1, Z + 1, sides)
    each(first, second, weight_block)

    def joined(dz):
        tz = wrap(z + dz, Z)
        value = mine[tz * Y + y, x].astype(f32)
        for dx in range(1, S):
            along_x(dx, tz).wait_recv()
            value = value + from_x[(dx - 1) * Z + tz].astype(f32)
        for dy in range(1, Y):
            along_y(dy, tz).wait_recv()
            value = value + from_y[(dy - 1) * Z + tz].astype(f32)
        return value

    def pass_on(dz):
        to_z[dz] = joined(dz).astype(bf16)
        along_z(dz).start()

    each(1, Z, pass_on)
    each(second, M, weight_block)
    value = joined(0)
    for dz in range(1, Z):
        along_z(dz).wait_recv()
        value = value + from_z[dz].astype(f32)
    out_ref[...] = value.astype(bf16)

    def sent(tz):
        for dy in range(Y):
            if C > 1:
                near_copy(tz * Y + dy).wait_send()
        for dx in range(1, S):
            along_x(dx, tz).wait_send()
            for dy in range(1, Y):
                half_a(dx, dy, tz).wait_send()
                half_b(dx, dy, tz).wait_send()
        for dy in range(1, Y):
            along_y(dy, tz).wait_send()

    each(0, Z, sent)
    each(1, Z, lambda dz: along_z(dz).wait_send())

    def written(p):
        put(p).wait()

    each(0, M, written)


def fused_kernel(
    grid, len_ref, enc_ref, w_ref, q_in, g_in,
    ctx_out, qgrad_out, enc_out, wgrad_out,
    kv, q, g, ctx, qgrad, prob, grad, kvgrad, local_sem,
    held, weight, raw, pick, total, raw_sem, send_sem, recv_sem,
    packed, mix, *rest,
):
    R = enc_ref.shape[0]

    def local(src, dst, i):
        return pltpu.make_async_copy(src, dst, local_sem.at[i])

    local(q_in, q, 0).start()
    local(g_in, g, 1).start()
    finish = gather(
        grid, enc_ref, w_ref, kv, held, weight, raw, pick, total, raw_sem, send_sem, recv_sem
    )
    local(q_in, q, 0).wait()
    local(g_in, g, 1).wait()
    each(
        0, grid.S,
        lambda m: attention_grads(m, R, len_ref, kv, q, g, prob, grad, kvgrad),
    )

    def while_moving():
        each(0, grid.S, lambda m: attention_outputs(m, R, kv, prob, grad, ctx, qgrad))
        local(ctx, ctx_out, 2).start()
        local(qgrad, qgrad_out, 3).start()

    scatter(grid, kvgrad, enc_out, wgrad_out, while_moving, weight, held, packed, mix, *rest)
    local(ctx, ctx_out, 2).wait()
    local(qgrad, qgrad_out, 3).wait()
    finish()


def settle_kernel(count, *refs):
    sources, targets, buffers = refs[:count], refs[count : 2 * count], refs[2 * count : -2]
    in_sem, out_sem = refs[-2:]
    plan = []
    for source, target, buffer in zip(sources, targets, buffers):
        axis = 1 if source.shape[0] < 16 else 0
        parts = 8 if source.shape[axis] % 128 == 0 else 1
        step = source.shape[axis] // parts
        for i in range(parts):
            rows = pl.ds(i * step, step)
            plan.append((source, target, buffer, (slice(None), rows) if axis else (rows,)))
    plan.reverse()

    def load(i):
        source, _, buffer, rows = plan[i]
        return pltpu.make_async_copy(source.at[rows], buffer.at[rows], in_sem.at[i])

    def store(i):
        _, target, buffer, rows = plan[i]
        return pltpu.make_async_copy(buffer.at[rows], target.at[rows], out_sem.at[i])

    for i in range(len(plan)):
        load(i).start()
    for i in range(len(plan)):
        load(i).wait()
        store(i).start()
    for i in range(len(plan)):
        store(i).wait()


def shards(grid, enc_final, enc_len, kv_weight, queries, d_context):
    S, M, C, Y, Z = grid.S, grid.M, grid.C, grid.Y, grid.Z
    R, F = enc_final.shape[1:]
    D, _, L = kv_weight.shape[1:]
    T = queries.shape[2]
    lane_tiles = L // LANES
    bf16, f32 = jnp.bfloat16, jnp.float32
    dma = pltpu.SemaphoreType.DMA
    vmem = pl.BlockSpec(memory_space=pltpu.VMEM)
    anywhere = pl.BlockSpec(memory_space=pl.ANY)
    shape = jax.ShapeDtypeStruct
    by_lane_tile = (
        kv_weight[0].reshape(D, 2, lane_tiles, LANES).transpose(0, 2, 1, 3)
    ).reshape(D * lane_tiles, 2, LANES)
    sends = Z + (S - 1) * Z + (Y - 1) * Z + 2 * (S - 1) * (Y - 1) * Z + S * Y * Z
    pair = max((S - 1) * (Y - 1) * Z, 1)
    heads = L // HD
    results = (
        shape((S, T, L), bf16), shape((S, T, L), bf16),
        shape((R, F), bf16), shape((D * lane_tiles, 2, LANES), bf16),
    )
    partial = pl.pallas_call(
        functools.partial(fused_kernel, grid),
        out_shape=results,
        in_specs=[pl.BlockSpec(memory_space=pltpu.SMEM), vmem, anywhere, anywhere, anywhere],
        out_specs=(anywhere, anywhere, vmem, anywhere),
        scratch_shapes=[
            pltpu.VMEM((S * R, 2 * L), bf16),
            pltpu.VMEM((S, T, L), bf16),
            pltpu.VMEM((S, T, L), bf16),
            pltpu.VMEM((S, T, L), bf16),
            pltpu.VMEM((S, T, L), bf16),
            pltpu.VMEM((S, heads * R, T), bf16),
            pltpu.VMEM((S, heads * R, T), bf16),
            pltpu.VMEM((S * R, 2 * L), bf16),
            dma((4,)),
            pltpu.VMEM((S, M, R, F), bf16),
            pltpu.VMEM((D, 2 * L), bf16),
            pltpu.VMEM((D * lane_tiles, 2, LANES), bf16),
            pltpu.VMEM((2 * LANES, 2 * LANES), bf16),
            pltpu.VMEM((S * R, 2 * L), f32),
            dma((4,)),
            dma((sends,)),
            dma((2, S, M)),
            pltpu.VMEM((M, F * lane_tiles, 2, LANES), bf16),
            pltpu.VMEM((2 * LANES, 2 * LANES), bf16),
            pltpu.VMEM((Z * Y, S, R, F), bf16),
            pltpu.VMEM((Z * Y, S, R, F), bf16),
            pltpu.VMEM((Z * Y, S, R, F), bf16),
            pltpu.VMEM((pair, R // 2, F), bf16),
            pltpu.VMEM((pair, R // 2, F), bf16),
            pltpu.VMEM((max(S - 1, 1) * Z, R, F), bf16),
            pltpu.VMEM((max(Y - 1, 1) * Z, R, F), bf16),
            pltpu.VMEM((Z, R, F), bf16),
            pltpu.VMEM((Z, R, F), bf16),
            dma((Z * Y,)), dma((Z * Y,)),
            dma((pair,)), dma((pair,)), dma((pair,)), dma((pair,)),
            dma((max(S - 1, 1) * Z,)), dma((max(S - 1, 1) * Z,)),
            dma((max(Y - 1, 1) * Z,)), dma((max(Y - 1, 1) * Z,)),
            dma((Z,)), dma((Z,)), dma((M,)),
        ],
        compiler_params=pltpu.CompilerParams(
            collective_id=0, has_side_effects=True, vmem_limit_bytes=VMEM_BYTES
        ),
        name="cross_attention",
    )(enc_len, enc_final[0], by_lane_tile, queries[0], d_context[0])

    context, query_grad, enc_grad, weight_grad = pl.pallas_call(
        functools.partial(settle_kernel, len(results)),
        out_shape=results,
        in_specs=[anywhere] * len(results),
        out_specs=(anywhere,) * len(results),
        scratch_shapes=[
            *(pltpu.VMEM(r.shape, r.dtype) for r in results),
            dma((8 * len(results),)),
            dma((8 * len(results),)),
        ],
        compiler_params=pltpu.CompilerParams(vmem_limit_bytes=VMEM_BYTES),
        name="settle_results",
    )(*partial)
    weight_grad = (
        weight_grad.reshape(D, lane_tiles, 2, LANES).transpose(0, 2, 1, 3).reshape(D, 2, L)
    )
    return context[None], query_grad[None], weight_grad[None], enc_grad[None]


def solution(mesh):
    grid = Grid(mesh.shape["section"], mesh.shape["mp"])
    split = P("section", None, None, "mp")
    return jax.shard_map(
        functools.partial(shards, grid),
        mesh=mesh,
        in_specs=(P("section", None, "mp"), P(), split, split, split),
        out_specs=(split, split, split, P("section", None, "mp")),
        check_vma=False,
    )
```
